256 devices in a mesh: hist: 4 (over y), ent: 64 (over x, z, core).
Axes of the slice: x: 4, y: 4, z: 8, core: 2. Of those that a mesh axis runs over, the one named last changes fastest.
Arguments:
- states: bfloat16 [4, 16384, 512], P('hist', 'ent'), may hold values from -6 to 6
- w_neigh: bfloat16 [2, 256, 256], replicated, may hold values from -0.375 to 0.375
- w_self: bfloat16 [512, 512], replicated, may hold values from -0.25 to 0.25
- w_gate: bfloat16 [512, 512], replicated, may hold values from -0.25 to 0.25
- b_gate: float32 [512], replicated, may hold values from -4 to 4
- relation: bfloat16 [460, 512], replicated, may hold values from -6 to 6
- edge_src: int32 [4, 32768], P('hist', 'ent'), may hold values from 0 to 255
- edge_rel: int32 [4, 32768], P('hist', 'ent'), may hold values from 0 to 459
- edge_dst: int32 [4, 32768], P('hist', 'ent'), may hold values from 0 to 255
- send_counts: int32 [4, 4096], P('hist', 'ent'), may hold values from 1 to 8, as said below
- query_ent: int32 [8192], P('ent'), may hold values from 0 to 255
- query_rel: int32 [8192], P('ent'), may hold values from 0 to 459
- query_grad: float32 [8192, 512], P('ent'), may hold values from -6 to 6
Outputs:
- grad_states: float32 [4, 16384, 512], P('hist', 'ent')
- grad_neigh: float32 [2, 256, 256], replicated
- grad_self: float32 [512, 512], replicated
- grad_gate: float32 [512, 512], replicated
- grad_bias: float32 [512], replicated
- grad_relation: float32 [460, 512], replicated
The draws below stay inside these ranges and needn't reach their ends.
Inputs may be any that keep to these rules, and one draw needn't show every extreme that they name: `send_counts`: slots at or beyond their bucket's count hold arbitrary ids and carry no edge. In every snapshot one target partition receives exactly 8 slots in use from every source partition; which one is drawn.
All inputs are finite; a program needn't handle non-finite values.
Results may differ from the reference program's by a relative error of at most 0.0053.
Values may be sent and summed in bfloat16 or wider, within the bound.
A program may use at most 64 MiB of HBM per device.

```python
import math
import jax
import jax.numpy as jnp
import numpy as np
from jax import lax

D = 512
NREL = 460
BLOCKS = 2
ENT_DEV = 256
EDGE_DEV = 512
Q_DEV = 128
HIST = 4
HALF = 256
CAP = 8
ENTITIES = 16384
EDGES = 32768
QUERIES = 8192
N_ENT = 64


def draw_send_counts(key, part):
    base_key, hot_key = jax.random.split(jax.random.fold_in(key, 17))
    filled = jax.random.randint(base_key, (HIST, N_ENT, N_ENT), CAP // 8, CAP + 1)
    hot_dest = jax.random.randint(hot_key, (HIST, 1, 1), 0, N_ENT)
    dest_index = lax.broadcasted_iota(jnp.int32, (HIST, N_ENT, N_ENT), 2)
    return jnp.where(dest_index == hot_dest, CAP, filled).reshape(HIST, N_ENT * N_ENT).astype(jnp.int32)


def plant(entries, stream_key, low, high):
    longest = entries.shape.index(max(entries.shape))
    spots = []
    for shift in (0, 1):
        where = [jax.random.randint(jax.random.fold_in(stream_key, axis), (), 0, length) for axis, length in enumerate(entries.shape)]
        where[longest] = (where[longest] + shift) % entries.shape[longest]
        spots.append(tuple(where))
    return entries.at[spots[0]].set(low).at[spots[1]].set(high)


def levels(stream_key, dims, shards, smallest, top_value):
    def one(position, parts):
        heights = jax.random.uniform(jax.random.fold_in(jax.random.fold_in(stream_key, 6), position), (parts,), jnp.float32, smallest / len(shards), top_value / len(shards))
        return jnp.repeat(jnp.exp(heights), dims[position] // parts).reshape((-1,) + (1,) * (len(dims) - position - 1))

    level = one(*shards[0])
    for cut in shards[1:]:
        level = level * one(*cut)
    return level


def cumulative_ranks(count, skew):
    weights = [(1 << 20) // math.isqrt(grade ** skew) + 1 for grade in range(1, count + 1)]
    deviation = 1 + sum(weights) // (1 << 30)
    return np.cumsum(np.array([max(1, weight // deviation) for weight in weights]))


def skewed_ids(rng, shape, amount, skew):
    grid = cumulative_ranks(amount, skew)
    lot = jax.random.randint(jax.random.fold_in(rng, 1), shape, 0, int(grid[amount - 1]))
    standing = jnp.searchsorted(jnp.asarray(grid, jnp.int32), lot, side="right")
    return jax.random.permutation(jax.random.fold_in(rng, 2), amount)[standing].astype(jnp.int32)


def centred(key, dims, scale, reach, shards=(), kind=jnp.bfloat16):
    factor_of = levels(key, dims, shards, -0.22, 0.18) if shards else 1.0
    values = jax.random.normal(key, dims, jnp.float32) * scale * factor_of
    return jnp.minimum(jnp.maximum(values, -reach), reach).astype(kind)


def setup_inputs(seed: int = 0) -> dict:
    streams_of = jax.random.split(jax.random.key(seed), 14)
    states = centred(streams_of[0], (HIST, ENTITIES, D), 1.0, 6.0, ((0, 4), (1, 64)))
    w_neigh = centred(streams_of[1], (BLOCKS, HALF, HALF), HALF ** -0.5, 0.375)
    w_self = centred(streams_of[2], (D, D), D ** -0.5, 0.25)
    w_gate = centred(streams_of[3], (D, D), D ** -0.5, 0.25)
    b_gate = centred(streams_of[4], (D,), 1.0, 4.0, (), jnp.float32)
    relation = centred(streams_of[5], (NREL, D), 1.0, 6.0)
    edge_src = plant(jax.random.randint(streams_of[6], (HIST, EDGES), 0, ENT_DEV), jax.random.fold_in(streams_of[6], 1), 0, ENT_DEV - 1).astype(jnp.int32)
    edge_rel = plant(skewed_ids(streams_of[7], (HIST, EDGES), NREL, 2), jax.random.fold_in(streams_of[7], 3), 0, NREL - 1).astype(jnp.int32)
    edge_dst = plant(jax.random.randint(streams_of[8], (HIST, EDGES), 0, ENT_DEV), jax.random.fold_in(streams_of[8], 1), 0, ENT_DEV - 1).astype(jnp.int32)
    send_counts = draw_send_counts(jax.random.fold_in(streams_of[13], 71), 0)
    query_ent = plant(jax.random.randint(streams_of[10], (QUERIES,), 0, ENT_DEV), jax.random.fold_in(streams_of[10], 1), 0, ENT_DEV - 1).astype(jnp.int32)
    query_rel = plant(skewed_ids(streams_of[11], (QUERIES,), NREL, 2), jax.random.fold_in(streams_of[11], 3), 0, NREL - 1).astype(jnp.int32)
    query_grad = centred(streams_of[12], (QUERIES, D), 1.0, 6.0, ((0, 64),), jnp.float32)
    return {"states": states, "w_neigh": w_neigh, "w_self": w_self, "w_gate": w_gate, "b_gate": b_gate, "relation": relation, "edge_src": edge_src, "edge_rel": edge_rel, "edge_dst": edge_dst, "send_counts": send_counts, "query_ent": query_ent, "query_rel": query_rel, "query_grad": query_grad}


def snapshot(hidden, cotangent, src_glob, rel_ids, dst_glob, in_use, w_neigh, w_self, w_gate, b_gate, relation):
    entities = hidden.shape[0]
    features = hidden.shape[1]
    blocks = w_neigh.shape[0]
    block_width = w_neigh.shape[1]
    edges_all = src_glob.shape[0]
    inputs = (hidden[src_glob].astype(jnp.float32) + relation[rel_ids].astype(jnp.float32)).astype(jnp.bfloat16)
    product = jnp.einsum('ebi,bij->ebj', inputs.reshape(edges_all, blocks, block_width).astype(jnp.float32), w_neigh.astype(jnp.float32))
    message = (product.reshape(edges_all, features) * in_use[:, None]).astype(jnp.bfloat16)
    indegree = jax.ops.segment_sum(in_use, dst_glob, num_segments=entities)
    scaling = 1.0 / jnp.maximum(indegree, 1.0)
    summed = jax.ops.segment_sum(message.astype(jnp.float32), dst_glob, num_segments=entities)
    pre_act = summed * scaling[:, None] + jnp.dot(hidden, w_self, preferred_element_type=jnp.float32)
    gate_open = jax.nn.sigmoid(jnp.dot(hidden, w_gate, preferred_element_type=jnp.float32) + b_gate)
    sigmoid_pre = jax.nn.sigmoid(pre_act)
    new_state = pre_act * sigmoid_pre
    keep_part = cotangent * (1.0 - gate_open)
    gate_term = cotangent * (new_state - hidden.astype(jnp.float32)) * gate_open * (1.0 - gate_open)
    gate_low = gate_term.astype(jnp.bfloat16)
    pre_term = cotangent * gate_open * (sigmoid_pre * (1.0 + pre_act * (1.0 - sigmoid_pre)))
    pre_low = pre_term.astype(jnp.bfloat16)
    grad_gate = jnp.dot(hidden.T, gate_low, preferred_element_type=jnp.float32)
    grad_bias = lax.optimization_barrier(jnp.sum(gate_term, axis=0))
    grad_self = jnp.dot(hidden.T, pre_low, preferred_element_type=jnp.float32)
    back_sum = keep_part + jnp.dot(gate_low, w_gate.T, preferred_element_type=jnp.float32)
    back_sum = back_sum + jnp.dot(pre_low, w_self.T, preferred_element_type=jnp.float32)
    replies = (pre_term[dst_glob] * scaling[dst_glob][:, None] * in_use[:, None]).astype(jnp.bfloat16)
    grad_neigh = jnp.einsum('ebi,ebj->bij', inputs.reshape(edges_all, blocks, block_width).astype(jnp.float32), replies.reshape(edges_all, blocks, block_width).astype(jnp.float32))
    spread = jnp.einsum('ebj,bij->ebi', replies.reshape(edges_all, blocks, block_width).astype(jnp.float32), w_neigh.astype(jnp.float32)).reshape(edges_all, features)
    back_sum = back_sum + jax.ops.segment_sum(spread, src_glob, num_segments=entities)
    grad_rel = jax.ops.segment_sum(spread, rel_ids, num_segments=relation.shape[0])
    return (back_sum, (grad_neigh, grad_self, grad_gate, grad_bias, grad_rel))

def reference(states, w_neigh, w_self, w_gate, b_gate, relation, edge_src, edge_rel, edge_dst, send_counts, query_ent, query_rel, query_grad):
    edge_pos = jnp.arange(EDGES, dtype=jnp.int32)
    part_of = edge_pos // EDGE_DEV
    bucket = edge_pos % EDGE_DEV // CAP
    within = edge_pos % CAP
    owners = jnp.arange(QUERIES, dtype=jnp.int32) // Q_DEV
    rows_glob = (owners * ENT_DEV + query_ent).astype(jnp.int32)
    top_grad = jnp.zeros((ENTITIES, D), jnp.float32).at[rows_glob].add(query_grad.astype(jnp.float32))
    cotangent = top_grad
    totals = None
    collected = []
    for step_index in range(HIST - 1, -1, -1):
        counts = send_counts[step_index][(part_of * N_ENT + bucket).astype(jnp.int32)]
        in_use = (within < counts).astype(jnp.float32)
        src_glob = (part_of * ENT_DEV + edge_src[step_index]).astype(jnp.int32)
        dst_glob = (bucket * ENT_DEV + edge_dst[step_index]).astype(jnp.int32)
        back_sum, grads = snapshot(states[step_index], cotangent, src_glob, edge_rel[step_index], dst_glob, in_use, w_neigh, w_self, w_gate, b_gate, relation)
        if totals is None:
            totals = grads
        else:
            totals = tuple((a + b for a, b in zip(totals, grads)))
        collected.append(back_sum)
        cotangent = back_sum
    grad_states = jnp.stack(collected[::-1], axis=0)
    grad_neigh, grad_self, grad_gate, grad_bias, grad_rel = totals
    grad_rel = grad_rel + jax.ops.segment_sum(query_grad.astype(jnp.float32), query_rel, num_segments=NREL)
    factor = 1.0 / jnp.sqrt(jnp.float32(HIST * ENTITIES))
    return (grad_states, grad_neigh * factor, grad_self * factor, grad_gate * factor, grad_bias * factor, grad_rel * factor)
```

```python
import functools
import math

import jax
import jax.numpy as jnp
from jax import lax
from jax.experimental import pallas as pl
from jax.experimental.pallas import tpu as pltpu
from jax.sharding import PartitionSpec as P

MESH = pl.DeviceIdType.MESH
bf16 = jnp.bfloat16
f32 = jnp.float32

HIST = 4
ENT = 64
CORES, XS, ZS = 2, 4, 8
ROWS = 256
D = 512
HALF = 256
SLOTS = 512
NREL = 460
REL_PAD = 512
REL_ROWS = 464
O_GATE = 0
O_SELF = 2048
O_NEIGH = 4096
O_REL = 5120
O_BIAS = O_REL + 4 * REL_ROWS
GROWS = 7168
CORE_ROWS = GROWS // CORES
X_ROWS = CORE_ROWS // XS
Z_ROWS = X_ROWS // ZS


def nn(a, b):
    return jnp.dot(a, b, preferred_element_type=f32)


def nt(a, b):
    return lax.dot_general(a, b, (((1,), (1,)), ((), ())), preferred_element_type=f32)


def tn(a, b):
    return lax.dot_general(a, b, (((0,), (0,)), ((), ())), preferred_element_type=f32)


def iota(shape, dim):
    return lax.broadcasted_iota(jnp.int32, shape, dim)


def hot(cond):
    return jnp.where(cond, 1.0, 0.0).astype(bf16)


def split(v):
    high = v.astype(bf16)
    return high, (v - high.astype(f32)).astype(bf16)


def pack(m):
    low = m[:, :128].reshape(ENT, 8, 128)
    high = m[:, 128:].reshape(ENT, 8, 128)
    return jnp.concatenate([low, high], axis=1).astype(bf16)


def unpack(r):
    wide = r.astype(f32)
    low = wide[:, :8, :].reshape(SLOTS, 128)
    high = wide[:, 8:, :].reshape(SLOTS, 128)
    return jnp.concatenate([low, high], axis=1).astype(bf16)


def kernel(
    factor,
    states,
    w_neigh,
    w_self,
    w_gate,
    b_gate,
    relation,
    edge_src,
    edge_rel,
    edge_dst,
    counts,
    query_ent,
    query_rel,
    query_grad,
    out_states,
    out_neigh,
    out_self,
    out_gate,
    out_bias,
    out_rel,
    id_send,
    id_recv,
    f_send,
    f_recv,
    b_send,
    b_recv,
    c_send,
    c_recv,
    rel_pad,
    inputs,
    hot_src_t,
    hot_rel_t,
    hot_dst,
    returned,
    cot,
    keep,
    coef_gate,
    coef_pre,
    scaling,
    gate_low,
    pre_low,
    base,
    grads,
    core_recv,
    x_send,
    x_recv,
    z_send,
    z_recv,
    y_send,
    y_recv,
    gathered,
    id_sem,
    f_sem,
    b_sem,
    c_sem,
    core_sem,
    x_sem,
    z_sem,
    y_sem,
    gz_sem,
    gx_sem,
    gc_sem,
):
    hist = lax.axis_index("hist")
    me = lax.axis_index("ent")
    core = lax.rem(me, CORES)
    z = lax.rem(me // CORES, ZS)
    x = me // (CORES * ZS)

    barrier = pltpu.get_barrier_semaphore()

    def greet(i, carry):
        pl.semaphore_signal(
            barrier, inc=1, device_id={"ent": lax.rem(me + i, ENT)}, device_id_type=MESH
        )
        return carry

    lax.fori_loop(1, ENT, greet, 0)
    for i in range(1, HIST):
        pl.semaphore_signal(
            barrier, inc=1, device_id={"hist": lax.rem(hist + i, HIST)}, device_id_type=MESH
        )

    dst = edge_dst[...].astype(f32)
    own_slot = jnp.where((iota((ENT, SLOTS), 1) >> 3) == iota((ENT, SLOTS), 0), dst, 0.0)
    to_lane = hot((iota((SLOTS, 128), 0) & 7) == iota((SLOTS, 128), 1))
    target = nn(own_slot.astype(bf16), to_lane)
    own_count = jnp.where(
        iota((ENT, ENT), 0) == iota((ENT, ENT), 1), counts[...].astype(f32), 0.0
    )
    limit = nn(own_count.astype(bf16), jnp.ones((ENT, 128), bf16))
    id_send[...] = jnp.where(iota((ENT, 128), 1).astype(f32) < limit, target, -1.0)

    hot_src_t[...] = hot(iota((ROWS, SLOTS), 0) == edge_src[...])
    hot_rel_t[...] = hot(iota((REL_PAD, SLOTS), 0) == edge_rel[...])
    rel_pad[NREL // 16 * 16 :, :] = jnp.zeros((REL_PAD - NREL // 16 * 16, D), bf16)
    rel_pad[:NREL, :] = relation[...]
    inputs[...] = (
        tn(hot_src_t[...], states[0]) + tn(hot_rel_t[...], rel_pad[...])
    ).astype(bf16)

    pl.semaphore_wait(barrier, ENT - 1 + HIST - 1)

    def send_ids(i, carry):
        peer = lax.rem(me + i, ENT)
        pltpu.make_async_remote_copy(
            src_ref=id_send.at[pl.ds(peer, 1)],
            dst_ref=id_recv.at[pl.ds(me, 1)],
            send_sem=id_sem.at[0],
            recv_sem=id_sem.at[1],
            device_id={"ent": peer},
            device_id_type=MESH,
        ).start()
        return carry

    lax.fori_loop(1, ENT, send_ids, 0)
    id_recv[pl.ds(me, 1), :] = id_send[pl.ds(me, 1), :]

    def exchange(send, recv, sem, b):
        def step(i, carry):
            peer = lax.rem(me + i, ENT)
            pltpu.make_async_remote_copy(
                src_ref=send.at[b, peer],
                dst_ref=recv.at[b, me],
                send_sem=sem.at[0, b],
                recv_sem=sem.at[1, b],
                device_id={"ent": peer},
                device_id_type=MESH,
            ).start()
            return carry

        lax.fori_loop(1, ENT, step, 0)
        recv[b, me] = send[b, me]

    def wait_all(ref, sem):
        pltpu.make_async_copy(ref.at[pl.ds(0, ENT - 1)], ref.at[pl.ds(0, ENT - 1)], sem).wait()

    for b in range(2):
        cols = slice(b * HALF, (b + 1) * HALF)
        f_send[b] = pack(nn(inputs[:, cols], w_neigh[b]))
        exchange(f_send, f_recv, f_sem, b)

    hidden = states[0]
    base[...] = nn(hidden, w_self[...])
    gate = jax.nn.sigmoid(nn(hidden, w_gate[...]) + b_gate[...])
    keep[...] = 1.0 - gate

    grads[O_BIAS:, :] = jnp.zeros((GROWS - O_BIAS, 128), f32)

    @pl.when(hist == HIST - 1)
    def _():
        hot_query = hot(iota((ROWS, 128), 0) == query_ent[...])
        q = query_grad[...]
        high = q.astype(bf16)
        rest = q - high.astype(f32)
        middle, low = split(rest)
        cot[...] = nn(hot_query, high) + (nn(hot_query, middle) + nn(hot_query, low))

    wait_all(id_recv, id_sem.at[1])
    to_slot = hot((iota((SLOTS, ENT), 0) >> 3) == iota((SLOTS, ENT), 1))
    arrived = nn(to_slot, id_recv[...].astype(bf16))
    arrived = jnp.where(
        iota((SLOTS, 128), 1) == (iota((SLOTS, 128), 0) & 7), arrived, 0.0
    ).astype(bf16)
    ones = jnp.ones((ROWS, 128), bf16)
    hot_dst[...] = hot(nt(arrived, ones) == iota((SLOTS, ROWS), 1).astype(f32))
    hot_dst_t = hot(nt(ones, arrived) == iota((ROWS, SLOTS), 0).astype(f32))
    degree = nn(hot_dst_t, jnp.ones((SLOTS, HALF), bf16))
    scaling[...] = 1.0 / jnp.maximum(degree, 1.0)

    for b in range(2):
        cols = slice(b * HALF, (b + 1) * HALF)
        wait_all(f_recv.at[b], f_sem.at[1, b])
        summed = nn(hot_dst_t, unpack(f_recv[b]))
        pre_act = summed * scaling[...] + base[:, cols]
        sig = jax.nn.sigmoid(pre_act)
        shut = keep[:, cols]
        opened = 1.0 - shut
        coef_gate[:, cols] = (pre_act * sig - states[0, :, cols].astype(f32)) * opened * shut
        coef_pre[:, cols] = opened * (sig * (1.0 + pre_act * (1.0 - sig)))

    for b in range(2):
        cols = slice(b * HALF, (b + 1) * HALF)

        @pl.when(hist < HIST - 1)
        def _():
            pltpu.make_async_copy(c_recv.at[b], c_recv.at[b], c_sem.at[1, b]).wait()
            cot[:, cols] = c_recv[b].astype(f32)

        c = cot[:, cols]
        pre_term = c * coef_pre[:, cols]
        b_send[b] = pack(nn(hot_dst[...], (pre_term * scaling[...]).astype(bf16)))
        exchange(b_send, b_recv, b_sem, b)
        pre_low[:, cols] = pre_term.astype(bf16)
        gate_term = c * coef_gate[:, cols]
        gate_low[:, cols] = gate_term.astype(bf16)
        bias = jnp.sum(gate_term, axis=0, keepdims=True)
        for j in range(2):
            at = O_BIAS + 2 * b + j
            grads[at : at + 1, :] = bias[:, j * 128 : (j + 1) * 128]

    base[...] = (
        cot[...] * keep[...] + nt(gate_low[...], w_gate[...]) + nt(pre_low[...], w_self[...])
    )
    for start, low in ((O_GATE, gate_low), (O_SELF, pre_low)):
        total = tn(hidden, low[...])
        for j in range(4):
            grads[start + j * 512 : start + (j + 1) * 512, :] = total[:, j * 128 : (j + 1) * 128]

    for b in range(2):
        cols = slice(b * HALF, (b + 1) * HALF)
        wait_all(b_recv.at[b], b_sem.at[1, b])
        back = unpack(b_recv[b])
        returned[:, cols] = back
        high, low = split(nn(hot_src_t[...], back))
        result = base[:, cols] + (nt(high, w_neigh[b]) + nt(low, w_neigh[b]))
        out_states[0, :, cols] = result

        @pl.when(hist > 0)
        def _():
            c_send[b] = result.astype(bf16)
            pltpu.make_async_remote_copy(
                src_ref=c_send.at[b],
                dst_ref=c_recv.at[b],
                send_sem=c_sem.at[0, b],
                recv_sem=c_sem.at[1, b],
                device_id={"hist": hist - 1},
                device_id_type=MESH,
            ).start()

    for b in range(2):
        cols = slice(b * HALF, (b + 1) * HALF)
        back = returned[:, cols]
        total = tn(inputs[:, cols], back)
        high, low = split(nn(hot_rel_t[...], back))
        by_rel = nt(high, w_neigh[b]) + nt(low, w_neigh[b])
        for j in range(2):
            lanes = slice(j * 128, (j + 1) * 128)
            at = O_NEIGH + (2 * b + j) * 256
            grads[at : at + 256, :] = total[:, lanes]
            at = O_REL + (2 * b + j) * REL_ROWS
            grads[at : at + REL_ROWS, :] = by_rel[:REL_ROWS, lanes]

    @pl.when(hist == HIST - 1)
    def _():
        hot_query = hot(iota((REL_PAD, 128), 0) == query_rel[...])
        q = query_grad[...]
        high = q.astype(bf16)
        rest = q - high.astype(f32)
        middle, low = split(rest)
        part = nn(hot_query, high) + (nn(hot_query, middle) + nn(hot_query, low))
        for j in range(4):
            at = O_REL + j * REL_ROWS
            grads[at : at + REL_ROWS, :] += part[:REL_ROWS, j * 128 : (j + 1) * 128]

    def remote(src, dst, sem, i, where):
        copy = pltpu.make_async_remote_copy(
            src_ref=src,
            dst_ref=dst,
            send_sem=sem.at[0, i],
            recv_sem=sem.at[1, i],
            device_id=where,
            device_id_type=MESH,
        )
        copy.start()
        return copy

    other = 1 - core
    partner = me + 1 - 2 * core
    core_copy = remote(
        grads.at[pl.ds(pl.multiple_of(other * CORE_ROWS, CORE_ROWS), CORE_ROWS)],
        core_recv,
        core_sem,
        0,
        {"ent": partner},
    )
    core_copy.wait()
    mine = pl.multiple_of(core * CORE_ROWS, CORE_ROWS)
    x_send[...] = (
        (grads[pl.ds(mine, CORE_ROWS), :] + core_recv[...]).astype(bf16).reshape(XS, X_ROWS, 128)
    )
    copies = []
    for i in range(1, XS):
        there = lax.rem(x + i, XS)
        copies.append(
            remote(
                x_send.at[there],
                x_recv.at[x],
                x_sem,
                i,
                {"ent": me + (there - x) * (CORES * ZS)},
            )
        )
    part_rows = pl.ds(pl.multiple_of(mine + x * X_ROWS, X_ROWS), X_ROWS)
    here = pl.ds(pl.multiple_of(x * X_ROWS, X_ROWS), X_ROWS)
    total = grads[part_rows, :] + core_recv[here, :]
    for copy in copies:
        copy.wait()
    for i in range(1, XS):
        total = total + x_recv[lax.rem(x + i, XS)].astype(f32)
    z_send[...] = total.astype(bf16).reshape(ZS, Z_ROWS, 128)
    z_recv[z] = z_send[z]
    copies = []
    for i in range(1, ZS):
        there = lax.rem(z + i, ZS)
        copies.append(
            remote(
                z_send.at[there], z_recv.at[z], z_sem, i, {"ent": me + (there - z) * CORES}
            )
        )
    for copy in copies:
        copy.wait()
    shard = z_recv[0].astype(f32)
    for i in range(1, ZS):
        shard = shard + z_recv[i].astype(f32)
    y_send[...] = shard
    copies = []
    for i in range(1, HIST):
        copies.append(
            remote(y_send, y_recv.at[hist], y_sem, i, {"hist": lax.rem(hist + i, HIST)})
        )
    y_recv[hist] = shard
    for copy in copies:
        copy.wait()
    shard = (y_recv[0] + y_recv[1]) + (y_recv[2] + y_recv[3])

    start = pl.multiple_of(mine + x * X_ROWS + z * Z_ROWS, Z_ROWS)
    own = gathered.at[pl.ds(start, Z_ROWS)]
    own[...] = shard.astype(bf16)
    copies = []
    for i in range(1, ZS):
        there = lax.rem(z + i, ZS)
        copies.append(remote(own, own, gz_sem, i, {"ent": me + (there - z) * CORES}))
    for copy in copies:
        copy.wait()
    own = gathered.at[part_rows]
    copies = []
    for i in range(1, XS):
        there = lax.rem(x + i, XS)
        copies.append(remote(own, own, gx_sem, i, {"ent": me + (there - x) * (CORES * ZS)}))
    for copy in copies:
        copy.wait()
    own = gathered.at[pl.ds(mine, CORE_ROWS)]
    remote(own, own, gc_sem, 0, {"ent": partner}).wait()

    for j in range(4):
        lanes = slice(j * 128, (j + 1) * 128)
        for ref, first, rows in (
            (out_gate, O_GATE, 512),
            (out_self, O_SELF, 512),
        ):
            at = first + j * rows
            ref[:, lanes] = gathered[at : at + rows, :].astype(f32) * factor
        at = O_NEIGH + j * 256
        out_neigh[j // 2, :, (j % 2) * 128 : (j % 2 + 1) * 128] = (
            gathered[at : at + 256, :].astype(f32) * factor
        )
        at = O_REL + j * REL_ROWS
        out_rel[:, lanes] = gathered[at : at + REL_ROWS, :].astype(f32)[:NREL] * factor
    bias = gathered[O_BIAS : O_BIAS + 16, :].astype(f32) * factor
    for j in range(4):
        out_bias[:, j * 128 : (j + 1) * 128] = bias[j : j + 1, :]

    wait_all(id_send, id_sem.at[0])
    for b in range(2):
        wait_all(f_send.at[b], f_sem.at[0, b])
        wait_all(b_send.at[b], b_sem.at[0, b])

        @pl.when(hist > 0)
        def _():
            pltpu.make_async_copy(c_send.at[b], c_send.at[b], c_sem.at[0, b]).wait()


def on_device(
    states,
    w_neigh,
    w_self,
    w_gate,
    b_gate,
    relation,
    edge_src,
    edge_rel,
    edge_dst,
    send_counts,
    query_ent,
    query_rel,
    query_grad,
):
    factor = 1.0 / math.sqrt(HIST * ENT * ROWS)
    vmem = pl.BlockSpec(memory_space=pltpu.VMEM)
    dma = pltpu.SemaphoreType.DMA
    shape = jax.ShapeDtypeStruct
    outs = pl.pallas_call(
        functools.partial(kernel, factor),
        out_shape=(
            shape((1, ROWS, D), f32),
            shape((2, HALF, HALF), f32),
            shape((D, D), f32),
            shape((D, D), f32),
            shape((1, D), f32),
            shape((NREL, D), f32),
        ),
        in_specs=[vmem] * 13,
        out_specs=(vmem,) * 6,
        scratch_shapes=[
            pltpu.VMEM((ENT, 128), f32),
            pltpu.VMEM((ENT, 128), f32),
            pltpu.VMEM((2, ENT, 16, 128), bf16),
            pltpu.VMEM((2, ENT, 16, 128), bf16),
            pltpu.VMEM((2, ENT, 16, 128), bf16),
            pltpu.VMEM((2, ENT, 16, 128), bf16),
            pltpu.VMEM((2, ROWS, HALF), bf16),
            pltpu.VMEM((2, ROWS, HALF), bf16),
            pltpu.VMEM((REL_PAD, D), bf16),
            pltpu.VMEM((SLOTS, D), bf16),
            pltpu.VMEM((ROWS, SLOTS), bf16),
            pltpu.VMEM((REL_PAD, SLOTS), bf16),
            pltpu.VMEM((SLOTS, ROWS), bf16),
            pltpu.VMEM((SLOTS, D), bf16),
            pltpu.VMEM((ROWS, D), f32),
            pltpu.VMEM((ROWS, D), f32),
            pltpu.VMEM((ROWS, D), f32),
            pltpu.VMEM((ROWS, D), f32),
            pltpu.VMEM((ROWS, HALF), f32),
            pltpu.VMEM((ROWS, D), bf16),
            pltpu.VMEM((ROWS, D), bf16),
            pltpu.VMEM((ROWS, D), f32),
            pltpu.VMEM((GROWS, 128), f32),
            pltpu.VMEM((CORE_ROWS, 128), f32),
            pltpu.VMEM((XS, X_ROWS, 128), bf16),
            pltpu.VMEM((XS, X_ROWS, 128), bf16),
            pltpu.VMEM((ZS, Z_ROWS, 128), bf16),
            pltpu.VMEM((ZS, Z_ROWS, 128), bf16),
            pltpu.VMEM((Z_ROWS, 128), f32),
            pltpu.VMEM((HIST, Z_ROWS, 128), f32),
            pltpu.VMEM((GROWS, 128), bf16),
            dma((2,)),
            dma((2, 2)),
            dma((2, 2)),
            dma((2, 2)),
            dma((2, 1)),
            dma((2, XS)),
            dma((2, ZS)),
            dma((2, HIST)),
            dma((2, ZS)),
            dma((2, XS)),
            dma((2, 1)),
        ],
        compiler_params=pltpu.CompilerParams(
            collective_id=0, has_side_effects=True, vmem_limit_bytes=50 << 20
        ),
        name="encoder_backward",
    )(
        states,
        w_neigh,
        w_self,
        w_gate,
        b_gate.reshape(1, D),
        relation,
        edge_src,
        edge_rel,
        edge_dst,
        send_counts,
        query_ent.reshape(1, 128),
        query_rel.reshape(1, 128),
        query_grad,
    )
    result, grad_neigh, grad_self, grad_gate, grad_bias, grad_rel = outs
    return result, grad_neigh, grad_self, grad_gate, grad_bias.reshape(D), grad_rel


def solution(mesh):
    return jax.shard_map(
        on_device,
        mesh=mesh,
        in_specs=(
            P("hist", "ent", None),
            P(),
            P(),
            P(),
            P(),
            P(),
            P("hist", "ent"),
            P("hist", "ent"),
            P("hist", "ent"),
            P("hist", "ent"),
            P("ent"),
            P("ent"),
            P("ent", None),
        ),
        out_specs=(P("hist", "ent", None), P(), P(), P(), P(), P()),
        check_vma=False,
    )
```

```python
import functools
import math

import jax
import jax.numpy as jnp
from jax import lax
from jax.experimental import pallas as pl
from jax.experimental.pallas import tpu as pltpu
from jax.sharding import PartitionSpec as P

MESH = pl.DeviceIdType.MESH
bf16 = jnp.bfloat16
f32 = jnp.float32

HIST = 4
ENT = 64
CORES, XS, ZS = 2, 4, 8
ROWS = 256
D = 512
HALF = 256
QUART = 128
SLOTS = 512
NREL = 460
REL_PAD = 512
R_GATE, R_SELF, R_NEIGH, R_REL, R_QUERY = 0, 8, 16, 24, 32
SHARD = 40
KEPT = 32
BIAS_ROW = 508


def nn(a, b):
    return jnp.dot(a, b, preferred_element_type=f32)


def nt(a, b):
    return lax.dot_general(a, b, (((1,), (1,)), ((), ())), preferred_element_type=f32)


def tn(a, b):
    return lax.dot_general(a, b, (((0,), (0,)), ((), ())), preferred_element_type=f32)


def iota(shape, dim):
    return lax.broadcasted_iota(jnp.int32, shape, dim)


def hot(cond):
    return jnp.where(cond, 1.0, 0.0).astype(bf16)


def split(v):
    high = v.astype(bf16)
    return high, (v - high.astype(f32)).astype(bf16)


def split3(v):
    high = v.astype(bf16)
    middle, low = split(v - high.astype(f32))
    return high, middle, low


def by_shard(v):
    return v.reshape(-1, 8, QUART)


def pack(m):
    return m.reshape(ENT, 8, QUART).astype(bf16)


def unpack(r):
    return r.astype(f32).reshape(SLOTS, QUART).astype(bf16)


def kernel(
    states_in,
    w_neigh_in,
    w_self_in,
    w_gate_in,
    b_gate_in,
    relation_in,
    edge_src_in,
    edge_rel_in,
    edge_dst_in,
    counts_in,
    query_ent_in,
    query_rel_in,
    query_grad_in,
    gathered,
    result,
    states,
    w_cols,
    w_own,
    w_other,
    w_self,
    w_gate,
    b_gate,
    relation,
    ids,
    edge_dst,
    counts,
    query_ent,
    query_rel,
    query_grad,
    id_send,
    id_recv,
    rel_block,
    inputs,
    hot_src_t,
    hot_rel_t,
    hot_dst,
    f_send,
    f_recv,
    b_send,
    b_recv,
    cot,
    keep,
    coef_gate,
    coef_pre,
    scaling,
    bias,
    part,
    part_send,
    part_recv,
    sum_send,
    sum_recv,
    res_send,
    grads,
    core_recv,
    x_send,
    x_recv,
    z_send,
    z_recv,
    rel_send,
    rel_recv,
    fetch_sem,
    id_sem,
    fwd_id_sem,
    st_sem,
    ids_sem,
    f_sem,
    b_sem,
    part_sem,
    sum_sem,
    res_sem,
    core_sem,
    x_sem,
    z_sem,
    rel_sem,
    gy_sem,
    gz_sem,
    gx_sem,
    gc_sem,
):
    hist = lax.axis_index("hist")
    me = lax.axis_index("ent")
    core = lax.rem(me, CORES)
    z = lax.rem(me // CORES, ZS)
    x = me // (CORES * ZS)
    block = hist // 2
    side = lax.rem(hist, 2)
    mate = hist + 1 - 2 * side

    top = HIST - 1
    barrier = pltpu.get_barrier_semaphore()

    def greet(i, carry):
        pl.semaphore_signal(
            barrier, inc=1, device_id={"ent": lax.rem(me + i, ENT)}, device_id_type=MESH
        )
        return carry

    cols = pl.ds(pl.multiple_of(hist * QUART, QUART), QUART)
    near = pl.ds(pl.multiple_of(side * QUART, QUART), QUART)
    far = pl.ds(pl.multiple_of((1 - side) * QUART, QUART), QUART)
    fetched = []

    def fetch(src, dst):
        copy = pltpu.make_async_copy(src, dst, fetch_sem.at[len(fetched)])
        copy.start()
        fetched.append(copy)

    fetch(edge_dst_in, edge_dst)
    fetch(counts_in, counts)
    fetch(edge_src_in, ids.at[hist, pl.ds(0, 1)])
    fetch(edge_rel_in, ids.at[hist, pl.ds(1, 1)])
    fetch(states_in.at[0, :, pl.ds(0, HALF)], states.at[hist, 0])
    fetch(states_in.at[0, :, pl.ds(HALF, HALF)], states.at[hist, 1])
    fetch(relation_in, relation)
    fetch(w_neigh_in.at[block, :, near], w_cols)
    fetch(w_neigh_in.at[block, near, near], w_own)
    fetch(w_neigh_in.at[block, near, far], w_other)
    fetch(w_self_in.at[:, cols], w_self)
    fetch(w_gate_in.at[:, cols], w_gate)
    fetch(b_gate_in.at[:, cols], b_gate)
    fetch(query_ent_in, query_ent)
    fetch(query_rel_in, query_rel)
    fetch(query_grad_in.at[:, cols], query_grad)

    lax.fori_loop(1, ENT, greet, 0)
    for i in range(1, HIST):
        pl.semaphore_signal(
            barrier, inc=1, device_id={"hist": lax.rem(hist + i, HIST)}, device_id_type=MESH
        )

    fetched[0].wait()
    fetched[1].wait()
    dst = edge_dst[...].astype(f32)
    own_slot = jnp.where((iota((ENT, SLOTS), 1) >> 3) == iota((ENT, SLOTS), 0), dst, 0.0)
    to_lane = hot((iota((SLOTS, 128), 0) & 7) == iota((SLOTS, 128), 1))
    target = nn(own_slot.astype(bf16), to_lane)
    own_count = jnp.where(
        iota((ENT, ENT), 0) == iota((ENT, ENT), 1), counts[...].astype(f32), 0.0
    )
    limit = nn(own_count.astype(bf16), jnp.ones((ENT, 128), bf16))
    id_send[...] = jnp.where(iota((ENT, 128), 1).astype(f32) < limit, target, -1.0)

    for i in range(2, 6):
        fetched[i].wait()

    def wait_bytes(ref, sem):
        pltpu.make_async_copy(ref, ref, sem).wait()

    def remote(src, dst, send, recv, where):
        copy = pltpu.make_async_remote_copy(
            src_ref=src,
            dst_ref=dst,
            send_sem=send,
            recv_sem=recv,
            device_id=where,
            device_id_type=MESH,
        )
        copy.start()
        return copy

    def share_states(t):
        @pl.when(hist == t)
        def _():
            order = [(t + 3) % HIST, (t + 1) % HIST, (t + 2) % HIST]
            for p in order:
                remote(
                    ids.at[t], ids.at[t], ids_sem.at[0, t], ids_sem.at[1, t], {"hist": p}
                )
            for first in (True, False):
                for p in order:
                    b = p // 2 if first else 1 - p // 2
                    remote(
                        states.at[t, b],
                        states.at[t, b],
                        st_sem.at[0, t],
                        st_sem.at[1 + b, t],
                        {"hist": p},
                    )

    pl.semaphore_wait(barrier, ENT - 1 + HIST - 1)
    share_states(HIST - 1)

    def send_ids(i, carry):
        peer = lax.rem(me + i, ENT)
        remote(
            id_send.at[pl.ds(peer, 1)],
            id_recv.at[hist, pl.ds(me, 1)],
            id_sem.at[0],
            id_sem.at[1],
            {"ent": peer},
        )
        return carry

    lax.fori_loop(1, ENT, send_ids, 0)
    id_recv[hist, pl.ds(me, 1), :] = id_send[pl.ds(me, 1), :]

    def exchange(send, recv, sem, t):
        def step(i, carry):
            peer = lax.rem(me + i, ENT)
            remote(send.at[t, peer], recv.at[t, me], sem.at[0, t], sem.at[1, t], {"ent": peer})
            return carry

        lax.fori_loop(1, ENT, step, 0)
        recv[t, me] = send[t, me]

    others = pl.ds(0, ENT - 1)

    for i in range(6, len(fetched)):
        fetched[i].wait()
    rel_block[NREL // 16 * 16 :, :] = jnp.zeros((REL_PAD - NREL // 16 * 16, HALF), bf16)
    rel_block[:NREL, :] = relation[:, pl.ds(pl.multiple_of(block * HALF, HALF), HALF)]

    q_parts = split3(query_grad[...])
    hot_query = hot(iota((ROWS, 128), 0) == query_ent[...])
    cot[...] = nn(hot_query, q_parts[0]) + (nn(hot_query, q_parts[1]) + nn(hot_query, q_parts[2]))
    hot_query = hot(iota((REL_PAD, 128), 0) == query_rel[...])
    grads[:, R_QUERY : R_QUERY + 8, :] = by_shard(
        nn(hot_query, q_parts[0]) + (nn(hot_query, q_parts[1]) + nn(hot_query, q_parts[2]))
    )
    grads[32:, R_NEIGH : R_NEIGH + 8, :] = jnp.zeros((32, 8, QUART), f32)

    def forward_messages(t):
        @pl.when(hist != t)
        def _():
            wait_bytes(ids.at[t], ids_sem.at[1, t])
            wait_bytes(states.at[t, block], st_sem.at[1 + block, t])

        if t == top:
            share_states(t - 1)
        hot_src_t[t] = hot(iota((ROWS, SLOTS), 0) == ids[t, 0:1, :])
        hot_rel_t[t] = hot(iota((REL_PAD, SLOTS), 0) == ids[t, 1:2, :])
        inputs[t] = (
            tn(hot_src_t[t], states[t, block]) + tn(hot_rel_t[t], rel_block[...])
        ).astype(bf16)
        f_send[t] = pack(nn(inputs[t], w_cols[...]))
        exchange(f_send, f_recv, f_sem, t)

    def forward_rest(t):
        @pl.when(hist != t)
        def _():
            wait_bytes(states.at[t, 1 - block], st_sem.at[2 - block, t])

        logit = nn(states[t, 0], w_gate[:HALF, :]) + nn(states[t, 1], w_gate[HALF:, :])
        dense = nn(states[t, 0], w_self[:HALF, :]) + nn(states[t, 1], w_self[HALF:, :])
        opened = jax.nn.sigmoid(logit + b_gate[...])
        shut = 1.0 - opened

        @pl.when(hist != t)
        def _():
            wait_bytes(id_recv.at[t], fwd_id_sem.at[1, t])

        to_slot = hot((iota((SLOTS, ENT), 0) >> 3) == iota((SLOTS, ENT), 1))
        arrived = nn(to_slot, id_recv[t].astype(bf16))
        arrived = jnp.where(
            iota((SLOTS, 128), 1) == (iota((SLOTS, 128), 0) & 7), arrived, 0.0
        ).astype(bf16)
        ones = jnp.ones((ROWS, 128), bf16)
        hot_dst[t] = hot(nt(arrived, ones) == iota((SLOTS, ROWS), 1).astype(f32))
        hot_dst_t = hot(nt(ones, arrived) == iota((ROWS, SLOTS), 0).astype(f32))
        degree = nn(hot_dst_t, jnp.ones((SLOTS, QUART), bf16))
        scale = 1.0 / jnp.maximum(degree, 1.0)
        scaling[t] = scale
        wait_bytes(f_recv.at[t, others], f_sem.at[1, t])
        pre_act = nn(hot_dst_t, unpack(f_recv[t])) * scale + dense
        sig = jax.nn.sigmoid(pre_act)
        keep[t] = shut
        own = states[t, block, :, near].astype(f32)
        coef_gate[t] = (pre_act * sig - own) * opened * shut
        coef_pre[t] = opened * (sig * (1.0 + pre_act * (1.0 - sig)))

    forward_messages(top)
    wait_bytes(id_recv.at[hist, others], id_sem.at[1])
    for i in range(1, HIST):
        remote(
            id_recv.at[hist],
            id_recv.at[hist],
            fwd_id_sem.at[0, hist],
            fwd_id_sem.at[1, hist],
            {"hist": lax.rem(hist + i, HIST)},
        )
    for t in range(top - 1):
        share_states(t)
    forward_rest(top)

    def add_grads(at, value, t, shards=ENT):
        if t == top:
            grads[:shards, at : at + 8, :] = by_shard(value)
        else:
            grads[:shards, at : at + 8, :] += by_shard(value)

    def returned_grads(t):
        back = unpack(b_recv[t])
        add_grads(R_NEIGH, tn(inputs[t], back), t, 32)
        add_grads(R_REL, nn(hot_rel_t[t], back), t)

    for t in range(top, -1, -1):
        c = cot[...]
        pre_term = c * coef_pre[t]
        b_send[t] = pack(nn(hot_dst[t], (pre_term * scaling[t]).astype(bf16)))
        exchange(b_send, b_recv, b_sem, t)
        gate_term = c * coef_gate[t]
        gate_low = gate_term.astype(bf16)
        pre_low = pre_term.astype(bf16)
        for j in range(4):
            rows = slice(j * QUART, (j + 1) * QUART)
            piece = nt(gate_low, w_gate[rows, :]) + nt(pre_low, w_self[rows, :])
            part[j] = piece
            part_send[t, j] = piece.astype(bf16)
        for i in range(1, HIST):
            there = lax.rem(hist + i, HIST)
            remote(
                part_send.at[t, there],
                part_recv.at[t, hist],
                part_sem.at[0, t],
                part_sem.at[1, t],
                {"hist": there},
            )
        if t > 0:
            forward_messages(t - 1)
        down = jnp.sum(gate_term, axis=0, keepdims=True)
        bias[...] = down if t == top else bias[...] + down
        for at, low in ((R_GATE, gate_low), (R_SELF, pre_low)):
            add_grads(
                at, jnp.concatenate([tn(states[t, 0], low), tn(states[t, 1], low)], axis=0), t
            )
        if t < top:
            returned_grads(t + 1)

        wait_bytes(b_recv.at[t, others], b_sem.at[1, t])
        high, low = split(nn(hot_src_t[t], unpack(b_recv[t])))
        sum_send[t] = high
        remote(
            sum_send.at[t], sum_recv.at[t], sum_sem.at[0, t], sum_sem.at[1, t], {"hist": mate}
        )
        near_part = nt(high, w_own[...]) + nt(low, w_own[...]) + c * keep[t] + part[hist]
        if t > 0:
            forward_rest(t - 1)
        wait_bytes(part_recv.at[t, pl.ds(0, HIST - 1)], part_sem.at[1, t])
        for i in range(1, HIST):
            near_part = near_part + part_recv[t, lax.rem(hist + i, HIST)].astype(f32)
        wait_bytes(sum_recv.at[t], sum_sem.at[1, t])
        c = near_part + nt(sum_recv[t], w_other[...])
        cot[...] = c
        res_send[t] = c.astype(bf16)

        @pl.when(hist == t)
        def _():
            result[t] = res_send[t]

        @pl.when(hist != t)
        def _():
            remote(
                res_send.at[t],
                result.at[hist],
                res_sem.at[0],
                res_sem.at[1],
                {"hist": t},
            )

    returned_grads(0)
    grads[BIAS_ROW // 8, R_QUERY + BIAS_ROW % 8 : R_QUERY + BIAS_ROW % 8 + 1, :] = bias[...]

    partner = me + 1 - 2 * core
    half = ENT // CORES
    mine = pl.multiple_of(core * half, half)
    remote(
        grads.at[pl.ds(pl.multiple_of((1 - core) * half, half), half)],
        core_recv,
        core_sem.at[0],
        core_sem.at[1],
        {"ent": partner},
    ).wait()
    x_send[...] = (grads[pl.ds(mine, half)] + core_recv[...]).astype(bf16).reshape(
        XS, ZS, SHARD, QUART
    )
    copies = []
    for i in range(1, XS):
        there = lax.rem(x + i, XS)
        copies.append(
            remote(
                x_send.at[there],
                x_recv.at[x],
                x_sem.at[0, i],
                x_sem.at[1, i],
                {"ent": me + (there - x) * (CORES * ZS)},
            )
        )
    total = grads[pl.ds(mine + x * ZS, ZS)] + core_recv[pl.ds(x * ZS, ZS)]
    for copy in copies:
        copy.wait()
    for i in range(1, XS):
        total = total + x_recv[lax.rem(x + i, XS)].astype(f32)
    z_send[...] = total
    copies = []
    for i in range(1, ZS):
        there = lax.rem(z + i, ZS)
        copies.append(
            remote(
                z_send.at[there],
                z_recv.at[z],
                z_sem.at[0, i],
                z_sem.at[1, i],
                {"ent": me + (there - z) * CORES},
            )
        )
    shard = z_send[z]
    for copy in copies:
        copy.wait()
    for i in range(1, ZS):
        shard = shard + z_recv[lax.rem(z + i, ZS)]

    rel_send[...] = shard[R_REL : R_REL + 8, :]
    remote(rel_send, rel_recv, rel_sem.at[0], rel_sem.at[1], {"hist": mate}).wait()
    by_rel = shard[R_QUERY : R_QUERY + 8, :]
    for v, w in ((rel_send[...], w_own), (rel_recv[...], w_other)):
        high = v.astype(bf16).astype(f32)
        both = nt(jnp.concatenate([high, v - high], axis=0).astype(bf16), w[...])
        by_rel = by_rel + (both[:8, :] + both[8:, :])

    place = mine + x * ZS + z
    gathered[place, hist] = jnp.concatenate([shard[:R_REL, :], by_rel], axis=0).astype(bf16)
    own = gathered.at[place, hist]
    copies = []
    for i in range(1, HIST):
        there = lax.rem(hist + i, HIST)
        copies.append(remote(own, own, gy_sem.at[0, i], gy_sem.at[1, i], {"hist": there}))
    for copy in copies:
        copy.wait()
    own = gathered.at[place]
    copies = []
    for i in range(1, ZS):
        there = lax.rem(z + i, ZS)
        copies.append(
            remote(own, own, gz_sem.at[0, i], gz_sem.at[1, i], {"ent": me + (there - z) * CORES})
        )
    for copy in copies:
        copy.wait()
    own = gathered.at[pl.ds(mine + x * ZS, ZS)]
    copies = []
    for i in range(1, XS):
        there = lax.rem(x + i, XS)
        copies.append(
            remote(
                own,
                own,
                gx_sem.at[0, i],
                gx_sem.at[1, i],
                {"ent": me + (there - x) * (CORES * ZS)},
            )
        )
    for copy in copies:
        copy.wait()
    own = gathered.at[pl.ds(mine, half)]
    remote(own, own, gc_sem.at[0], gc_sem.at[1], {"ent": partner}).wait()

    three = pl.ds(0, HIST - 1)
    wait_bytes(result.at[three], res_sem.at[1])
    wait_bytes(res_send.at[three], res_sem.at[0])
    wait_bytes(id_send.at[others], id_sem.at[0])
    wait_bytes(id_recv.at[three], fwd_id_sem.at[0, hist])
    wait_bytes(ids.at[three], ids_sem.at[0, hist])
    wait_bytes(states.at[three], st_sem.at[0, hist])
    for t in range(HIST):
        wait_bytes(f_send.at[t, others], f_sem.at[0, t])
        wait_bytes(b_send.at[t, others], b_sem.at[0, t])
        wait_bytes(part_send.at[t, three], part_sem.at[0, t])
        wait_bytes(sum_send.at[t], sum_sem.at[0, t])


def unfold(factor, gathered, result, out_states, out_neigh, out_self, out_gate, out_bias, out_rel):
    for h in range(HIST):
        lanes = slice(h * QUART, (h + 1) * QUART)
        out_states[0, :, lanes] = result[h].astype(f32)
        rows = gathered[:, h].astype(f32) * factor
        out_gate[:, lanes] = rows[:, R_GATE : R_GATE + 8, :].reshape(D, QUART)
        out_self[:, lanes] = rows[:, R_SELF : R_SELF + 8, :].reshape(D, QUART)
        out_neigh[h // 2, :, (h % 2) * QUART : (h % 2 + 1) * QUART] = rows[
            :32, R_NEIGH : R_NEIGH + 8, :
        ].reshape(HALF, QUART)
        by_rel = rows[:, R_REL : R_REL + 8, :].reshape(REL_PAD, QUART)
        out_rel[:, lanes] = by_rel[:NREL, :]
        out_bias[:, lanes] = by_rel[BIAS_ROW : BIAS_ROW + 1, :]


def on_device(
    states,
    w_neigh,
    w_self,
    w_gate,
    b_gate,
    relation,
    edge_src,
    edge_rel,
    edge_dst,
    send_counts,
    query_ent,
    query_rel,
    query_grad,
):
    factor = 1.0 / math.sqrt(HIST * ENT * ROWS)
    vmem = pl.BlockSpec(memory_space=pltpu.VMEM)
    anywhere = pl.BlockSpec(memory_space=pl.ANY)
    dma = pltpu.SemaphoreType.DMA
    shape = jax.ShapeDtypeStruct
    v = pltpu.VMEM
    i32 = jnp.int32
    gathered, result = pl.pallas_call(
        kernel,
        out_shape=(
            shape((ENT, HIST, KEPT, QUART), bf16),
            shape((HIST, ROWS, QUART), bf16),
        ),
        in_specs=[anywhere] * 13,
        out_specs=(vmem,) * 2,
        scratch_shapes=[
            v((HIST, 2, ROWS, HALF), bf16),
            v((HALF, QUART), bf16),
            v((QUART, QUART), bf16),
            v((QUART, QUART), bf16),
            v((D, QUART), bf16),
            v((D, QUART), bf16),
            v((1, QUART), f32),
            v((NREL, D), bf16),
            v((HIST, 8, SLOTS), i32),
            v((1, SLOTS), i32),
            v((1, ENT), i32),
            v((1, 128), i32),
            v((1, 128), i32),
            v((128, QUART), f32),
            v((ENT, 128), f32),
            v((HIST, ENT, 128), f32),
            v((REL_PAD, HALF), bf16),
            v((HIST, SLOTS, HALF), bf16),
            v((HIST, ROWS, SLOTS), bf16),
            v((HIST, REL_PAD, SLOTS), bf16),
            v((HIST, SLOTS, ROWS), bf16),
            v((HIST, ENT, 8, QUART), bf16),
            v((HIST, ENT, 8, QUART), bf16),
            v((HIST, ENT, 8, QUART), bf16),
            v((HIST, ENT, 8, QUART), bf16),
            v((ROWS, QUART), f32),
            v((HIST, ROWS, QUART), f32),
            v((HIST, ROWS, QUART), f32),
            v((HIST, ROWS, QUART), f32),
            v((HIST, ROWS, QUART), f32),
            v((1, QUART), f32),
            v((HIST, ROWS, QUART), f32),
            v((HIST, HIST, ROWS, QUART), bf16),
            v((HIST, HIST, ROWS, QUART), bf16),
            v((HIST, ROWS, QUART), bf16),
            v((HIST, ROWS, QUART), bf16),
            v((HIST, ROWS, QUART), bf16),
            v((ENT, SHARD, QUART), f32),
            v((ENT // CORES, SHARD, QUART), f32),
            v((XS, ZS, SHARD, QUART), bf16),
            v((XS, ZS, SHARD, QUART), bf16),
            v((ZS, SHARD, QUART), f32),
            v((ZS, SHARD, QUART), f32),
            v((8, QUART), f32),
            v((8, QUART), f32),
            dma((16,)),
            dma((2,)),
            dma((2, HIST)),
            dma((3, HIST)),
            dma((2, HIST)),
            dma((2, HIST)),
            dma((2, HIST)),
            dma((2, HIST)),
            dma((2, HIST)),
            dma((2,)),
            dma((2,)),
            dma((2, XS)),
            dma((2, ZS)),
            dma((2,)),
            dma((2, HIST)),
            dma((2, ZS)),
            dma((2, XS)),
            dma((2,)),
        ],
        compiler_params=pltpu.CompilerParams(
            collective_id=0, has_side_effects=True, vmem_limit_bytes=50 << 20
        ),
        name="encoder_backward",
    )(
        states,
        w_neigh,
        w_self,
        w_gate,
        b_gate.reshape(1, D),
        relation,
        edge_src,
        edge_rel,
        edge_dst,
        send_counts,
        query_ent.reshape(1, 128),
        query_rel.reshape(1, 128),
        query_grad,
    )
    result, grad_neigh, grad_self, grad_gate, grad_bias, grad_rel = pl.pallas_call(
        functools.partial(unfold, factor),
        out_shape=(
            shape((1, ROWS, D), f32),
            shape((2, HALF, HALF), f32),
            shape((D, D), f32),
            shape((D, D), f32),
            shape((1, D), f32),
            shape((NREL, D), f32),
        ),
        in_specs=[vmem] * 2,
        out_specs=(vmem,) * 6,
        compiler_params=pltpu.CompilerParams(vmem_limit_bytes=32 << 20),
        name="unfold",
    )(gathered, result)
    return result, grad_neigh, grad_self, grad_gate, grad_bias.reshape(D), grad_rel


def solution(mesh):
    return jax.shard_map(
        on_device,
        mesh=mesh,
        in_specs=(
            P("hist", "ent", None),
            P(),
            P(),
            P(),
            P(),
            P(),
            P("hist", "ent"),
            P("hist", "ent"),
            P("hist", "ent"),
            P("hist", "ent"),
            P("ent"),
            P("ent"),
            P("ent", None),
        ),
        out_specs=(P("hist", "ent", None), P(), P(), P(), P(), P()),
        check_vma=False,
    )
```

```python
import functools
import math

import jax
import jax.numpy as jnp
from jax import lax
from jax.experimental import pallas as pl
from jax.experimental.pallas import tpu as pltpu
from jax.sharding import PartitionSpec as P

MESH = pl.DeviceIdType.MESH
bf16 = jnp.bfloat16
f32 = jnp.float32

HIST = 4
ENT = 64
CORES, XS, ZS = 2, 4, 8
ROWS = 256
D = 512
HALF = 256
QUART = 128
SLOTS = 512
NREL = 460
REL_PAD = 512
R_GATE, R_SELF, R_QUERY, ROWS1 = 0, 8, 16, 24
R_NEIGH, R_REL, ROWS2 = 0, 8, 16
KEPT = 16
BIAS_ROW = 508
GROUP = ENT // CORES


def nn(a, b):
    return jnp.dot(a, b, preferred_element_type=f32)


def nt(a, b):
    return lax.dot_general(a, b, (((1,), (1,)), ((), ())), preferred_element_type=f32)


def tn(a, b):
    return lax.dot_general(a, b, (((0,), (0,)), ((), ())), preferred_element_type=f32)


def iota(shape, dim):
    return lax.broadcasted_iota(jnp.int32, shape, dim)


def hot(cond):
    return jnp.where(cond, 1.0, 0.0).astype(bf16)


def split(v):
    high = v.astype(bf16)
    return high, (v - high.astype(f32)).astype(bf16)


def split3(v):
    high = v.astype(bf16)
    middle, low = split(v - high.astype(f32))
    return high, middle, low


def by_shard(v):
    return v.reshape(-1, 8, QUART)


def pack(m):
    return m.reshape(ENT, 8, QUART).astype(bf16)


def unpack(r):
    return r.astype(f32).reshape(SLOTS, QUART).astype(bf16)


def kernel(
    states_in,
    w_neigh_in,
    w_self_in,
    w_gate_in,
    b_gate_in,
    relation_in,
    edge_src_in,
    edge_rel_in,
    edge_dst_in,
    counts_in,
    query_ent_in,
    query_rel_in,
    query_grad_in,
    gathered1,
    gathered2,
    result,
    states,
    w_cols,
    w_own,
    w_other,
    w_self,
    w_gate,
    b_gate,
    relation,
    ids,
    edge_dst,
    counts,
    query_ent,
    query_rel,
    query_grad,
    id_send,
    id_recv,
    rel_block,
    inputs,
    hot_src_t,
    hot_rel_t,
    hot_dst,
    f_send,
    f_recv,
    b_send,
    b_recv,
    cot,
    keep,
    coef_gate,
    coef_pre,
    scaling,
    bias,
    part,
    part_send,
    part_recv,
    sum_send,
    sum_recv,
    res_send,
    w_neigh,
    grads1,
    core_recv1,
    sum1,
    x_send1,
    x_recv1,
    z_send1,
    z_recv1,
    grads2,
    core_recv2,
    sum2,
    x_send2,
    x_recv2,
    z_send2,
    z_recv2,
    y_recv2,
    fetch_sem,
    id_sem,
    fwd_id_sem,
    st_sem,
    ids_sem,
    f_sem,
    b_sem,
    part_sem,
    sum_sem,
    res_sem,
    core_sem,
    x1_sem,
    z1_sem,
    x2_sem,
    z2_sem,
    y2_sem,
    gx1_sem,
    gz1_sem,
    gy1_sem,
    gc1_sem,
    gz2_sem,
    gx2_sem,
    gc2_sem,
):
    hist = lax.axis_index("hist")
    me = lax.axis_index("ent")
    core = lax.rem(me, CORES)
    z = lax.rem(me // CORES, ZS)
    x = me // (CORES * ZS)
    block = hist // 2
    side = lax.rem(hist, 2)
    mate = hist + 1 - 2 * side

    top = HIST - 1
    barrier = pltpu.get_barrier_semaphore()

    def greet(i, carry):
        pl.semaphore_signal(
            barrier, inc=1, device_id={"ent": lax.rem(me + i, ENT)}, device_id_type=MESH
        )
        return carry

    cols = pl.ds(pl.multiple_of(hist * QUART, QUART), QUART)
    near = pl.ds(pl.multiple_of(side * QUART, QUART), QUART)
    far = pl.ds(pl.multiple_of((1 - side) * QUART, QUART), QUART)
    fetched = []

    def fetch(src, dst):
        copy = pltpu.make_async_copy(src, dst, fetch_sem.at[len(fetched)])
        copy.start()
        fetched.append(copy)

    fetch(edge_dst_in, edge_dst)
    fetch(counts_in, counts)
    fetch(edge_src_in, ids.at[hist, pl.ds(0, 1)])
    fetch(edge_rel_in, ids.at[hist, pl.ds(1, 1)])
    fetch(states_in.at[0, :, pl.ds(0, HALF)], states.at[hist, 0])
    fetch(states_in.at[0, :, pl.ds(HALF, HALF)], states.at[hist, 1])
    fetch(relation_in, relation)
    fetch(w_neigh_in.at[block, :, near], w_cols)
    fetch(w_neigh_in.at[block, near, near], w_own)
    fetch(w_neigh_in.at[block, near, far], w_other)
    fetch(w_self_in.at[:, cols], w_self)
    fetch(w_gate_in.at[:, cols], w_gate)
    fetch(b_gate_in.at[:, cols], b_gate)
    fetch(query_ent_in, query_ent)
    fetch(query_rel_in, query_rel)
    fetch(query_grad_in.at[:, cols], query_grad)
    fetch(w_neigh_in, w_neigh)

    lax.fori_loop(1, ENT, greet, 0)
    for i in range(1, HIST):
        pl.semaphore_signal(
            barrier, inc=1, device_id={"hist": lax.rem(hist + i, HIST)}, device_id_type=MESH
        )

    fetched[0].wait()
    fetched[1].wait()
    dst = edge_dst[...].astype(f32)
    own_slot = jnp.where((iota((ENT, SLOTS), 1) >> 3) == iota((ENT, SLOTS), 0), dst, 0.0)
    to_lane = hot((iota((SLOTS, 128), 0) & 7) == iota((SLOTS, 128), 1))
    target = nn(own_slot.astype(bf16), to_lane)
    own_count = jnp.where(
        iota((ENT, ENT), 0) == iota((ENT, ENT), 1), counts[...].astype(f32), 0.0
    )
    limit = nn(own_count.astype(bf16), jnp.ones((ENT, 128), bf16))
    id_send[...] = jnp.where(iota((ENT, 128), 1).astype(f32) < limit, target, -1.0)

    for i in range(2, 6):
        fetched[i].wait()

    def wait_bytes(ref, sem):
        pltpu.make_async_copy(ref, ref, sem).wait()

    def remote(src, dst, send, recv, where):
        copy = pltpu.make_async_remote_copy(
            src_ref=src,
            dst_ref=dst,
            send_sem=send,
            recv_sem=recv,
            device_id=where,
            device_id_type=MESH,
        )
        copy.start()
        return copy

    def share_states(t):
        @pl.when(hist == t)
        def _():
            order = [(t + 3) % HIST, (t + 1) % HIST, (t + 2) % HIST]
            for p in order:
                remote(
                    ids.at[t], ids.at[t], ids_sem.at[0, t], ids_sem.at[1, t], {"hist": p}
                )
            for first in (True, False):
                for p in order:
                    b = p // 2 if first else 1 - p // 2
                    remote(
                        states.at[t, b],
                        states.at[t, b],
                        st_sem.at[0, t],
                        st_sem.at[1 + b, t],
                        {"hist": p},
                    )

    pl.semaphore_wait(barrier, ENT - 1 + HIST - 1)
    share_states(HIST - 1)

    def send_ids(i, carry):
        peer = lax.rem(me + i, ENT)
        remote(
            id_send.at[pl.ds(peer, 1)],
            id_recv.at[hist, pl.ds(me, 1)],
            id_sem.at[0],
            id_sem.at[1],
            {"ent": peer},
        )
        return carry

    lax.fori_loop(1, ENT, send_ids, 0)
    id_recv[hist, pl.ds(me, 1), :] = id_send[pl.ds(me, 1), :]

    def exchange(send, recv, sem, t):
        def step(i, carry):
            peer = lax.rem(me + i, ENT)
            remote(send.at[t, peer], recv.at[t, me], sem.at[0, t], sem.at[1, t], {"ent": peer})
            return carry

        lax.fori_loop(1, ENT, step, 0)
        recv[t, me] = send[t, me]

    others = pl.ds(0, ENT - 1)

    for i in range(6, len(fetched)):
        fetched[i].wait()
    rel_block[NREL // 16 * 16 :, :] = jnp.zeros((REL_PAD - NREL // 16 * 16, HALF), bf16)
    rel_block[:NREL, :] = relation[:, pl.ds(pl.multiple_of(block * HALF, HALF), HALF)]

    q_parts = split3(query_grad[...])
    hot_query = hot(iota((ROWS, 128), 0) == query_ent[...])
    cot[...] = nn(hot_query, q_parts[0]) + (nn(hot_query, q_parts[1]) + nn(hot_query, q_parts[2]))
    hot_query = hot(iota((REL_PAD, 128), 0) == query_rel[...])
    by_query = nn(hot_query, q_parts[0]) + (nn(hot_query, q_parts[1]) + nn(hot_query, q_parts[2]))
    for g in range(ENT):
        c, xx, zz = g // GROUP, g // ZS % XS, g % ZS
        at = c * GROUP + zz * XS + xx
        grads1[at, R_QUERY : R_QUERY + 8, :] = by_query[g * 8 : (g + 1) * 8, :]
    grads2[GROUP:, R_NEIGH : R_NEIGH + 8, :] = jnp.zeros((GROUP, 8, QUART), f32)

    def forward_messages(t):
        @pl.when(hist != t)
        def _():
            wait_bytes(ids.at[t], ids_sem.at[1, t])
            wait_bytes(states.at[t, block], st_sem.at[1 + block, t])

        if t == top:
            share_states(t - 1)
        hot_src_t[t] = hot(iota((ROWS, SLOTS), 0) == ids[t, 0:1, :])
        hot_rel_t[t] = hot(iota((REL_PAD, SLOTS), 0) == ids[t, 1:2, :])
        inputs[t] = (
            tn(hot_src_t[t], states[t, block]) + tn(hot_rel_t[t], rel_block[...])
        ).astype(bf16)
        f_send[t] = pack(nn(inputs[t], w_cols[...]))
        exchange(f_send, f_recv, f_sem, t)

    def forward_rest(t):
        @pl.when(hist != t)
        def _():
            wait_bytes(states.at[t, 1 - block], st_sem.at[2 - block, t])

        logit = nn(states[t, 0], w_gate[:HALF, :]) + nn(states[t, 1], w_gate[HALF:, :])
        dense = nn(states[t, 0], w_self[:HALF, :]) + nn(states[t, 1], w_self[HALF:, :])
        opened = jax.nn.sigmoid(logit + b_gate[...])
        shut = 1.0 - opened

        @pl.when(hist != t)
        def _():
            wait_bytes(id_recv.at[t], fwd_id_sem.at[1, t])

        to_slot = hot((iota((SLOTS, ENT), 0) >> 3) == iota((SLOTS, ENT), 1))
        arrived = nn(to_slot, id_recv[t].astype(bf16))
        arrived = jnp.where(
            iota((SLOTS, 128), 1) == (iota((SLOTS, 128), 0) & 7), arrived, 0.0
        ).astype(bf16)
        ones = jnp.ones((ROWS, 128), bf16)
        hot_dst[t] = hot(nt(arrived, ones) == iota((SLOTS, ROWS), 1).astype(f32))
        hot_dst_t = hot(nt(ones, arrived) == iota((ROWS, SLOTS), 0).astype(f32))
        degree = nn(hot_dst_t, jnp.ones((SLOTS, QUART), bf16))
        scale = 1.0 / jnp.maximum(degree, 1.0)
        scaling[t] = scale
        wait_bytes(f_recv.at[t, others], f_sem.at[1, t])
        pre_act = nn(hot_dst_t, unpack(f_recv[t])) * scale + dense
        sig = jax.nn.sigmoid(pre_act)
        keep[t] = shut
        own = states[t, block, :, near].astype(f32)
        coef_gate[t] = (pre_act * sig - own) * opened * shut
        coef_pre[t] = opened * (sig * (1.0 + pre_act * (1.0 - sig)))

    forward_messages(top)
    wait_bytes(id_recv.at[hist, others], id_sem.at[1])
    for i in range(1, HIST):
        remote(
            id_recv.at[hist],
            id_recv.at[hist],
            fwd_id_sem.at[0, hist],
            fwd_id_sem.at[1, hist],
            {"hist": lax.rem(hist + i, HIST)},
        )
    for t in range(top - 1):
        share_states(t)
    forward_rest(top)

    def add_grads(ref, at, value, t, owners=ENT):
        if t == top:
            ref[:owners, at : at + 8, :] = by_shard(value)
        else:
            ref[:owners, at : at + 8, :] += by_shard(value)

    def returned_grads(t):
        back = unpack(b_recv[t])
        add_grads(grads2, R_NEIGH, tn(inputs[t], back), t, GROUP)
        add_grads(grads2, R_REL, nn(hot_rel_t[t], back), t)

    partner = me + 1 - 2 * core
    mine = pl.multiple_of(core * GROUP, GROUP)
    half = pl.ds(mine, GROUP)
    other_half = pl.ds(pl.multiple_of((1 - core) * GROUP, GROUP), GROUP)

    def along_x(src, dst, sem):
        copies = []
        for i in range(1, XS):
            there = lax.rem(x + i, XS)
            where = {"ent": me + (there - x) * (CORES * ZS)}
            copies.append(remote(src(there), dst, sem.at[0, i], sem.at[1, i], where))
        return copies

    def along_z(src, dst, sem):
        copies = []
        for i in range(1, ZS):
            there = lax.rem(z + i, ZS)
            where = {"ent": me + (there - z) * CORES}
            copies.append(remote(src(there), dst, sem.at[0, i], sem.at[1, i], where))
        return copies

    def along_hist(src, dst, sem):
        copies = []
        for i in range(1, HIST):
            where = {"hist": lax.rem(hist + i, HIST)}
            copies.append(remote(src, dst, sem.at[0, i], sem.at[1, i], where))
        return copies

    def to_core(src, dst, sem, i):
        return remote(src, dst, sem.at[0, i], sem.at[1, i], {"ent": partner})

    def finish(copies):
        for copy in copies:
            copy.wait()

    for t in range(top, -1, -1):
        c = cot[...]
        pre_term = c * coef_pre[t]
        b_send[t] = pack(nn(hot_dst[t], (pre_term * scaling[t]).astype(bf16)))
        exchange(b_send, b_recv, b_sem, t)
        gate_term = c * coef_gate[t]
        gate_low = gate_term.astype(bf16)
        pre_low = pre_term.astype(bf16)
        for j in range(4):
            rows = slice(j * QUART, (j + 1) * QUART)
            piece = nt(gate_low, w_gate[rows, :]) + nt(pre_low, w_self[rows, :])
            part[j] = piece
            part_send[t, j] = piece.astype(bf16)
        for i in range(1, HIST):
            there = lax.rem(hist + i, HIST)
            remote(
                part_send.at[t, there],
                part_recv.at[t, hist],
                part_sem.at[0, t],
                part_sem.at[1, t],
                {"hist": there},
            )
        if t > 0:
            forward_messages(t - 1)
        down = jnp.sum(gate_term, axis=0, keepdims=True)
        bias[...] = down if t == top else bias[...] + down
        for at, low in ((R_GATE, gate_low), (R_SELF, pre_low)):
            total = jnp.concatenate([tn(states[t, 0], low), tn(states[t, 1], low)], axis=0)
            add_grads(grads1, at, total, t)
        if t == 0:
            row = R_QUERY + BIAS_ROW % 8
            grads1[BIAS_ROW // 8, row : row + 1, :] = bias[...]
            core1 = to_core(grads1.at[other_half], core_recv1, core_sem, 0)
        if t < top:
            returned_grads(t + 1)
        if t == 0:
            core1.wait()
            both = (grads1[half] + core_recv1[...]).reshape(ZS, XS, ROWS1, QUART)
            sum1[...] = both
            for xx in range(XS):
                x_send1[xx] = both[:, xx].astype(bf16)
            x1 = along_x(lambda there: x_send1.at[there], x_recv1.at[x], x1_sem)

        wait_bytes(b_recv.at[t, others], b_sem.at[1, t])
        high, low = split(nn(hot_src_t[t], unpack(b_recv[t])))
        sum_send[t] = high
        remote(
            sum_send.at[t], sum_recv.at[t], sum_sem.at[0, t], sum_sem.at[1, t], {"hist": mate}
        )
        near_part = nt(high, w_own[...]) + nt(low, w_own[...]) + c * keep[t] + part[hist]
        if t > 0:
            forward_rest(t - 1)
        else:
            returned_grads(0)
            core2 = to_core(grads2.at[other_half], core_recv2, core_sem, 1)
            finish(x1)
            total = sum1[:, x]
            for i in range(1, XS):
                total = total + x_recv1[lax.rem(x + i, XS)].astype(f32)
            z_send1[...] = total
            z1 = along_z(lambda there: z_send1.at[there], z_recv1.at[z], z1_sem)
        wait_bytes(part_recv.at[t, pl.ds(0, HIST - 1)], part_sem.at[1, t])
        for i in range(1, HIST):
            near_part = near_part + part_recv[t, lax.rem(hist + i, HIST)].astype(f32)
        wait_bytes(sum_recv.at[t], sum_sem.at[1, t])
        c = near_part + nt(sum_recv[t], w_other[...])
        cot[...] = c
        res_send[t] = c.astype(bf16)

        @pl.when(hist == t)
        def _():
            result[t] = res_send[t]

        @pl.when(hist != t)
        def _():
            remote(
                res_send.at[t],
                result.at[hist],
                res_sem.at[0],
                res_sem.at[1],
                {"hist": t},
            )

    core2.wait()
    both = (grads2[half] + core_recv2[...]).reshape(XS, ZS, ROWS2, QUART)
    sum2[...] = both
    x_send2[...] = both.astype(bf16)
    x2 = along_x(lambda there: x_send2.at[there], x_recv2.at[x], x2_sem)

    finish(z1)
    shard1 = z_send1[z]
    for i in range(1, ZS):
        shard1 = shard1 + z_recv1[lax.rem(z + i, ZS)]
    place1 = mine + z * XS + x
    gathered1[hist, place1] = shard1[:KEPT, :].astype(bf16)
    own1 = gathered1.at[hist, place1]
    gx1 = along_x(lambda there: own1, own1, gx1_sem)

    finish(x2)
    total = sum2[x]
    for i in range(1, XS):
        total = total + x_recv2[lax.rem(x + i, XS)].astype(f32)
    z_send2[...] = total
    z2 = along_z(lambda there: z_send2.at[there], z_recv2.at[z], z2_sem)

    finish(gx1)
    line1 = gathered1.at[hist, pl.ds(mine + z * XS, XS)]
    gz1 = along_z(lambda there: line1, line1, gz1_sem)

    finish(z2)
    shard2 = z_send2[z]
    for i in range(1, ZS):
        shard2 = shard2 + z_recv2[lax.rem(z + i, ZS)]
    y_recv2[hist] = jnp.concatenate([shard2, shard1[R_QUERY:, :]], axis=0)
    y2 = along_hist(y_recv2.at[hist], y_recv2.at[hist], y2_sem)

    finish(gz1)
    plane1 = gathered1.at[hist, half]
    last1 = [to_core(plane1, plane1, gc1_sem, 0)]
    gy1 = along_hist(plane1, plane1, gy1_sem)

    finish(y2)
    place2 = mine + x * ZS + z
    for b in range(2):
        wide = jnp.concatenate(
            [y_recv2[2 * b, R_REL : R_REL + 8, :], y_recv2[2 * b + 1, R_REL : R_REL + 8, :]], axis=1
        )
        high = wide.astype(bf16).astype(f32)
        twice = nt(jnp.concatenate([high, wide - high], axis=0).astype(bf16), w_neigh[b])
        by_rel = twice[:8, :] + twice[8:, :]
        for j in range(2):
            h = 2 * b + j
            rel_rows = by_rel[:, j * QUART : (j + 1) * QUART] + y_recv2[h, ROWS2:, :]
            gathered2[place2, h] = jnp.concatenate(
                [y_recv2[h, R_NEIGH : R_NEIGH + 8, :], rel_rows], axis=0
            ).astype(bf16)
    own2 = gathered2.at[place2]
    gz2 = along_z(lambda there: own2, own2, gz2_sem)
    finish(gz2)
    line2 = gathered2.at[pl.ds(mine + x * ZS, ZS)]
    gx2 = along_x(lambda there: line2, line2, gx2_sem)
    last2 = [to_core(line2, line2, gc2_sem, 0)]
    for i in range(1, HIST):
        gy1[i - 1].wait()
        came = gathered1.at[lax.rem(hist + HIST - i, HIST), half]
        last1.append(to_core(came, came, gc1_sem, i))
    for i in range(1, XS):
        gx2[i - 1].wait()
        came = gathered2.at[pl.ds(mine + lax.rem(x + XS - i, XS) * ZS, ZS)]
        last2.append(to_core(came, came, gc2_sem, i))
    finish(last1)
    finish(last2)

    three = pl.ds(0, HIST - 1)
    wait_bytes(result.at[three], res_sem.at[1])
    wait_bytes(res_send.at[three], res_sem.at[0])
    wait_bytes(id_send.at[others], id_sem.at[0])
    wait_bytes(id_recv.at[three], fwd_id_sem.at[0, hist])
    wait_bytes(ids.at[three], ids_sem.at[0, hist])
    wait_bytes(states.at[three], st_sem.at[0, hist])
    for t in range(HIST):
        wait_bytes(f_send.at[t, others], f_sem.at[0, t])
        wait_bytes(b_send.at[t, others], b_sem.at[0, t])
        wait_bytes(part_send.at[t, three], part_sem.at[0, t])
        wait_bytes(sum_send.at[t], sum_sem.at[0, t])


def unfold(
    factor,
    gathered1,
    gathered2,
    result,
    out_states,
    out_neigh,
    out_self,
    out_gate,
    out_bias,
    out_rel,
):
    for h in range(HIST):
        lanes = slice(h * QUART, (h + 1) * QUART)
        out_states[0, :, lanes] = result[h].astype(f32)
        rows = gathered1[h].astype(f32) * factor
        out_gate[:, lanes] = rows[:, R_GATE : R_GATE + 8, :].reshape(D, QUART)
        out_self[:, lanes] = rows[:, R_SELF : R_SELF + 8, :].reshape(D, QUART)
        rows = gathered2[:, h].astype(f32) * factor
        out_neigh[h // 2, :, (h % 2) * QUART : (h % 2 + 1) * QUART] = rows[
            :GROUP, R_NEIGH : R_NEIGH + 8, :
        ].reshape(HALF, QUART)
        by_rel = rows[:, R_REL : R_REL + 8, :].reshape(REL_PAD, QUART)
        out_rel[:, lanes] = by_rel[:NREL, :]
        out_bias[:, lanes] = by_rel[BIAS_ROW : BIAS_ROW + 1, :]


def on_device(
    states,
    w_neigh,
    w_self,
    w_gate,
    b_gate,
    relation,
    edge_src,
    edge_rel,
    edge_dst,
    send_counts,
    query_ent,
    query_rel,
    query_grad,
):
    factor = 1.0 / math.sqrt(HIST * ENT * ROWS)
    vmem = pl.BlockSpec(memory_space=pltpu.VMEM)
    anywhere = pl.BlockSpec(memory_space=pl.ANY)
    dma = pltpu.SemaphoreType.DMA
    shape = jax.ShapeDtypeStruct
    v = pltpu.VMEM
    i32 = jnp.int32
    gathered1, gathered2, result = pl.pallas_call(
        kernel,
        out_shape=(
            shape((HIST, ENT, KEPT, QUART), bf16),
            shape((ENT, HIST, KEPT, QUART), bf16),
            shape((HIST, ROWS, QUART), bf16),
        ),
        in_specs=[anywhere] * 13,
        out_specs=(vmem,) * 3,
        scratch_shapes=[
            v((HIST, 2, ROWS, HALF), bf16),
            v((HALF, QUART), bf16),
            v((QUART, QUART), bf16),
            v((QUART, QUART), bf16),
            v((D, QUART), bf16),
            v((D, QUART), bf16),
            v((1, QUART), f32),
            v((NREL, D), bf16),
            v((HIST, 8, SLOTS), i32),
            v((1, SLOTS), i32),
            v((1, ENT), i32),
            v((1, 128), i32),
            v((1, 128), i32),
            v((128, QUART), f32),
            v((ENT, 128), f32),
            v((HIST, ENT, 128), f32),
            v((REL_PAD, HALF), bf16),
            v((HIST, SLOTS, HALF), bf16),
            v((HIST, ROWS, SLOTS), bf16),
            v((HIST, REL_PAD, SLOTS), bf16),
            v((HIST, SLOTS, ROWS), bf16),
            v((HIST, ENT, 8, QUART), bf16),
            v((HIST, ENT, 8, QUART), bf16),
            v((HIST, ENT, 8, QUART), bf16),
            v((HIST, ENT, 8, QUART), bf16),
            v((ROWS, QUART), f32),
            v((HIST, ROWS, QUART), f32),
            v((HIST, ROWS, QUART), f32),
            v((HIST, ROWS, QUART), f32),
            v((HIST, ROWS, QUART), f32),
            v((1, QUART), f32),
            v((HIST, ROWS, QUART), f32),
            v((HIST, HIST, ROWS, QUART), bf16),
            v((HIST, HIST, ROWS, QUART), bf16),
            v((HIST, ROWS, QUART), bf16),
            v((HIST, ROWS, QUART), bf16),
            v((HIST, ROWS, QUART), bf16),
            v((2, HALF, HALF), bf16),
            v((ENT, ROWS1, QUART), f32),
            v((GROUP, ROWS1, QUART), f32),
            v((ZS, XS, ROWS1, QUART), f32),
            v((XS, ZS, ROWS1, QUART), bf16),
            v((XS, ZS, ROWS1, QUART), bf16),
            v((ZS, ROWS1, QUART), f32),
            v((ZS, ROWS1, QUART), f32),
            v((ENT, ROWS2, QUART), f32),
            v((GROUP, ROWS2, QUART), f32),
            v((XS, ZS, ROWS2, QUART), f32),
            v((XS, ZS, ROWS2, QUART), bf16),
            v((XS, ZS, ROWS2, QUART), bf16),
            v((ZS, ROWS2, QUART), f32),
            v((ZS, ROWS2, QUART), f32),
            v((HIST, ROWS2 + 8, QUART), f32),
            dma((17,)),
            dma((2,)),
            dma((2, HIST)),
            dma((3, HIST)),
            dma((2, HIST)),
            dma((2, HIST)),
            dma((2, HIST)),
            dma((2, HIST)),
            dma((2, HIST)),
            dma((2,)),
            dma((2, 2)),
            dma((2, XS)),
            dma((2, ZS)),
            dma((2, XS)),
            dma((2, ZS)),
            dma((2, HIST)),
            dma((2, XS)),
            dma((2, ZS)),
            dma((2, HIST)),
            dma((2, HIST)),
            dma((2, ZS)),
            dma((2, XS)),
            dma((2, XS)),
        ],
        compiler_params=pltpu.CompilerParams(
            collective_id=0, has_side_effects=True, vmem_limit_bytes=54 << 20
        ),
        name="encoder_backward",
    )(
        states,
        w_neigh,
        w_self,
        w_gate,
        b_gate.reshape(1, D),
        relation,
        edge_src,
        edge_rel,
        edge_dst,
        send_counts,
        query_ent.reshape(1, 128),
        query_rel.reshape(1, 128),
        query_grad,
    )
    result, grad_neigh, grad_self, grad_gate, grad_bias, grad_rel = pl.pallas_call(
        functools.partial(unfold, factor),
        out_shape=(
            shape((1, ROWS, D), f32),
            shape((2, HALF, HALF), f32),
            shape((D, D), f32),
            shape((D, D), f32),
            shape((1, D), f32),
            shape((NREL, D), f32),
        ),
        in_specs=[vmem] * 3,
        out_specs=(vmem,) * 6,
        compiler_params=pltpu.CompilerParams(vmem_limit_bytes=32 << 20),
        name="unfold",
    )(gathered1, gathered2, result)
    return result, grad_neigh, grad_self, grad_gate, grad_bias.reshape(D), grad_rel


def solution(mesh):
    return jax.shard_map(
        on_device,
        mesh=mesh,
        in_specs=(
            P("hist", "ent", None),
            P(),
            P(),
            P(),
            P(),
            P(),
            P("hist", "ent"),
            P("hist", "ent"),
            P("hist", "ent"),
            P("hist", "ent"),
            P("ent"),
            P("ent"),
            P("ent", None),
        ),
        out_specs=(P("hist", "ent", None), P(), P(), P(), P(), P()),
        check_vma=False,
    )
```

```python
import functools
import math

import jax
import jax.numpy as jnp
from jax import lax
from jax.experimental import pallas as pl
from jax.experimental.pallas import tpu as pltpu
from jax.sharding import PartitionSpec as P

MESH = pl.DeviceIdType.MESH
bf16 = jnp.bfloat16
f32 = jnp.float32

HIST = 4
ENT = 64
CORES, XS, ZS = 2, 4, 8
ROWS = 256
D = 512
HALF = 256
QUART = 128
SLOTS = 512
NREL = 460
REL_PAD = 512
R_GATE, R_SELF, R_QUERY, ROWS1 = 0, 8, 16, 24
R_NEIGH, R_REL, ROWS2 = 0, 8, 16
KEPT = 16
BIAS_ROW = 508
GROUP = ENT // CORES


def nn(a, b):
    return jnp.dot(a, b, preferred_element_type=f32)


def nt(a, b):
    return lax.dot_general(a, b, (((1,), (1,)), ((), ())), preferred_element_type=f32)


def tn(a, b):
    return lax.dot_general(a, b, (((0,), (0,)), ((), ())), preferred_element_type=f32)


def iota(shape, dim):
    return lax.broadcasted_iota(jnp.int32, shape, dim)


def hot(cond):
    return jnp.where(cond, 1.0, 0.0).astype(bf16)


def split(v):
    high = v.astype(bf16)
    return high, (v - high.astype(f32)).astype(bf16)


def split3(v):
    high = v.astype(bf16)
    middle, low = split(v - high.astype(f32))
    return high, middle, low


def by_shard(v):
    return v.reshape(-1, 8, QUART)


def pack(m):
    return m.reshape(ENT, 8, QUART).astype(bf16)


def unpack(r):
    return r.astype(f32).reshape(SLOTS, QUART).astype(bf16)


def kernel(
    states_in,
    w_neigh_in,
    w_self_in,
    w_gate_in,
    b_gate_in,
    relation_in,
    edge_src_in,
    edge_rel_in,
    edge_dst_in,
    counts_in,
    query_ent_in,
    query_rel_in,
    query_grad_in,
    gathered1,
    gathered2,
    gathered3,
    result,
    states,
    w_cols,
    w_own,
    w_other,
    w_self,
    w_gate,
    b_gate,
    relation,
    ids,
    edge_dst,
    counts,
    query_ent,
    query_rel,
    query_grad,
    id_send,
    id_recv,
    rel_block,
    inputs,
    hot_src_t,
    hot_rel_t,
    hot_dst,
    f_send,
    f_recv,
    b_send,
    b_recv,
    cot,
    keep,
    coef_gate,
    coef_pre,
    scaling,
    bias,
    part,
    part_send,
    part_recv,
    sum_send,
    sum_recv,
    res_send,
    w_neigh,
    grads1,
    core_recv1,
    sum1,
    x_send1,
    x_recv1,
    z_send1,
    z_recv1,
    grads2,
    core_recv2,
    sum2,
    x_send2,
    x_recv2,
    z_send2,
    z_recv2,
    y_recv2,
    fetch_sem,
    id_sem,
    fwd_id_sem,
    st_sem,
    ids_sem,
    f_sem,
    b_sem,
    part_sem,
    sum_sem,
    res_sem,
    core_sem,
    x1_sem,
    z1_sem,
    x2_sem,
    z2_sem,
    y2_sem,
    gx1_sem,
    gz1_sem,
    gy1_sem,
    gc1_sem,
    gz2_sem,
    gx2_sem,
    gc2_sem,
    gx3_sem,
    gz3_sem,
    gy3_sem,
    gc3_sem,
):
    hist = lax.axis_index("hist")
    me = lax.axis_index("ent")
    core = lax.rem(me, CORES)
    z = lax.rem(me // CORES, ZS)
    x = me // (CORES * ZS)
    block = hist // 2
    side = lax.rem(hist, 2)
    mate = hist + 1 - 2 * side

    top = HIST - 1
    barrier = pltpu.get_barrier_semaphore()

    def greet(i, carry):
        pl.semaphore_signal(
            barrier, inc=1, device_id={"ent": lax.rem(me + i, ENT)}, device_id_type=MESH
        )
        return carry

    lax.fori_loop(1, ENT, greet, 0)
    for i in range(1, HIST):
        pl.semaphore_signal(
            barrier, inc=1, device_id={"hist": lax.rem(hist + i, HIST)}, device_id_type=MESH
        )

    cols = pl.ds(pl.multiple_of(hist * QUART, QUART), QUART)
    near = pl.ds(pl.multiple_of(side * QUART, QUART), QUART)
    far = pl.ds(pl.multiple_of((1 - side) * QUART, QUART), QUART)
    fetched = []

    def fetch(src, dst):
        copy = pltpu.make_async_copy(src, dst, fetch_sem.at[len(fetched)])
        copy.start()
        fetched.append(copy)

    fetch(edge_dst_in, edge_dst)
    fetch(counts_in, counts)
    fetch(edge_src_in, ids.at[hist, pl.ds(0, 1)])
    fetch(edge_rel_in, ids.at[hist, pl.ds(1, 1)])
    fetch(states_in.at[0, :, pl.ds(0, HALF)], states.at[hist, 0])
    fetch(states_in.at[0, :, pl.ds(HALF, HALF)], states.at[hist, 1])
    fetch(relation_in, relation)
    fetch(w_neigh_in.at[block, :, near], w_cols)
    fetch(w_neigh_in.at[block, near, near], w_own)
    fetch(w_neigh_in.at[block, near, far], w_other)
    fetch(w_self_in.at[:, cols], w_self)
    fetch(w_gate_in.at[:, cols], w_gate)
    fetch(b_gate_in.at[:, cols], b_gate)
    fetch(query_ent_in, query_ent)
    fetch(query_rel_in, query_rel)
    fetch(query_grad_in.at[:, cols], query_grad)
    fetch(w_neigh_in, w_neigh)

    fetched[0].wait()
    fetched[1].wait()
    dst = edge_dst[...].astype(f32)
    own_slot = jnp.where((iota((ENT, SLOTS), 1) >> 3) == iota((ENT, SLOTS), 0), dst, 0.0)
    to_lane = hot((iota((SLOTS, 128), 0) & 7) == iota((SLOTS, 128), 1))
    target = nn(own_slot.astype(bf16), to_lane)
    own_count = jnp.where(
        iota((ENT, ENT), 0) == iota((ENT, ENT), 1), counts[...].astype(f32), 0.0
    )
    limit = nn(own_count.astype(bf16), jnp.ones((ENT, 128), bf16))
    id_send[...] = jnp.where(iota((ENT, 128), 1).astype(f32) < limit, target, -1.0)

    for i in range(2, 6):
        fetched[i].wait()

    def wait_bytes(ref, sem):
        pltpu.make_async_copy(ref, ref, sem).wait()

    def remote(src, dst, send, recv, where):
        copy = pltpu.make_async_remote_copy(
            src_ref=src,
            dst_ref=dst,
            send_sem=send,
            recv_sem=recv,
            device_id=where,
            device_id_type=MESH,
        )
        copy.start()
        return copy

    def share_states(t):
        @pl.when(hist == t)
        def _():
            order = [(t + 3) % HIST, (t + 1) % HIST, (t + 2) % HIST]
            for p in order:
                remote(
                    ids.at[t], ids.at[t], ids_sem.at[0, t], ids_sem.at[1, t], {"hist": p}
                )
            for first in (True, False):
                for p in order:
                    b = p // 2 if first else 1 - p // 2
                    remote(
                        states.at[t, b],
                        states.at[t, b],
                        st_sem.at[0, t],
                        st_sem.at[1 + b, t],
                        {"hist": p},
                    )

    pl.semaphore_wait(barrier, ENT - 1 + HIST - 1)
    share_states(HIST - 1)

    def send_ids(i, carry):
        peer = lax.rem(me + i, ENT)
        remote(
            id_send.at[pl.ds(peer, 1)],
            id_recv.at[hist, pl.ds(me, 1)],
            id_sem.at[0],
            id_sem.at[1],
            {"ent": peer},
        )
        return carry

    lax.fori_loop(1, ENT, send_ids, 0)
    id_recv[hist, pl.ds(me, 1), :] = id_send[pl.ds(me, 1), :]

    def exchange(send, recv, sem, t):
        def step(i, carry):
            peer = lax.rem(me + i, ENT)
            remote(send.at[t, peer], recv.at[t, me], sem.at[0, t], sem.at[1, t], {"ent": peer})
            return carry

        lax.fori_loop(1, ENT, step, 0)
        recv[t, me] = send[t, me]

    others = pl.ds(0, ENT - 1)

    for i in range(6, len(fetched)):
        fetched[i].wait()
    rel_block[NREL // 16 * 16 :, :] = jnp.zeros((REL_PAD - NREL // 16 * 16, HALF), bf16)
    rel_block[:NREL, :] = relation[:, pl.ds(pl.multiple_of(block * HALF, HALF), HALF)]

    q_parts = split3(query_grad[...])
    hot_query = hot(iota((ROWS, 128), 0) == query_ent[...])
    cot[...] = nn(hot_query, q_parts[0]) + (nn(hot_query, q_parts[1]) + nn(hot_query, q_parts[2]))
    hot_query = hot(iota((REL_PAD, 128), 0) == query_rel[...])
    by_query = nn(hot_query, q_parts[0]) + (nn(hot_query, q_parts[1]) + nn(hot_query, q_parts[2]))
    for g in range(ENT):
        c, xx, zz = g // GROUP, g // ZS % XS, g % ZS
        at = c * GROUP + zz * XS + xx
        grads1[at, R_QUERY : R_QUERY + 8, :] = by_query[g * 8 : (g + 1) * 8, :]
    grads2[GROUP:, R_NEIGH : R_NEIGH + 8, :] = jnp.zeros((GROUP, 8, QUART), f32)

    def forward_messages(t):
        @pl.when(hist != t)
        def _():
            wait_bytes(ids.at[t], ids_sem.at[1, t])
            wait_bytes(states.at[t, block], st_sem.at[1 + block, t])

        if t == top:
            for later in range(t - 1, -1, -1):
                share_states(later)
        hot_src_t[t] = hot(iota((ROWS, SLOTS), 0) == ids[t, 0:1, :])
        hot_rel_t[t] = hot(iota((REL_PAD, SLOTS), 0) == ids[t, 1:2, :])
        inputs[t] = (
            tn(hot_src_t[t], states[t, block]) + tn(hot_rel_t[t], rel_block[...])
        ).astype(bf16)
        f_send[t] = pack(nn(inputs[t], w_cols[...]))
        exchange(f_send, f_recv, f_sem, t)

    def forward_rest(t):
        @pl.when(hist != t)
        def _():
            wait_bytes(states.at[t, 1 - block], st_sem.at[2 - block, t])

        logit = nn(states[t, 0], w_gate[:HALF, :]) + nn(states[t, 1], w_gate[HALF:, :])
        dense = nn(states[t, 0], w_self[:HALF, :]) + nn(states[t, 1], w_self[HALF:, :])
        opened = jax.nn.sigmoid(logit + b_gate[...])
        shut = 1.0 - opened

        @pl.when(hist != t)
        def _():
            wait_bytes(id_recv.at[t], fwd_id_sem.at[1, t])

        to_slot = hot((iota((SLOTS, ENT), 0) >> 3) == iota((SLOTS, ENT), 1))
        arrived = nn(to_slot, id_recv[t].astype(bf16))
        arrived = jnp.where(
            iota((SLOTS, 128), 1) == (iota((SLOTS, 128), 0) & 7), arrived, 0.0
        ).astype(bf16)
        ones = jnp.ones((ROWS, 128), bf16)
        hot_dst[t] = hot(nt(arrived, ones) == iota((SLOTS, ROWS), 1).astype(f32))
        hot_dst_t = hot(nt(ones, arrived) == iota((ROWS, SLOTS), 0).astype(f32))
        degree = nn(hot_dst_t, jnp.ones((SLOTS, QUART), bf16))
        scale = 1.0 / jnp.maximum(degree, 1.0)
        scaling[t] = scale
        wait_bytes(f_recv.at[t, others], f_sem.at[1, t])
        pre_act = nn(hot_dst_t, unpack(f_recv[t])) * scale + dense
        sig = jax.nn.sigmoid(pre_act)
        keep[t] = shut
        own = states[t, block, :, near].astype(f32)
        coef_gate[t] = (pre_act * sig - own) * opened * shut
        coef_pre[t] = opened * (sig * (1.0 + pre_act * (1.0 - sig)))

    forward_messages(top)
    wait_bytes(id_recv.at[hist, others], id_sem.at[1])
    for i in range(1, HIST):
        remote(
            id_recv.at[hist],
            id_recv.at[hist],
            fwd_id_sem.at[0, hist],
            fwd_id_sem.at[1, hist],
            {"hist": lax.rem(hist + i, HIST)},
        )
    forward_rest(top)

    def add_grads(ref, at, value, t, owners=ENT):
        if t == top:
            ref[:owners, at : at + 8, :] = by_shard(value)
        else:
            ref[:owners, at : at + 8, :] += by_shard(value)

    def returned_grads(t):
        back = unpack(b_recv[t])
        add_grads(grads2, R_NEIGH, tn(inputs[t], back), t, GROUP)
        add_grads(grads2, R_REL, nn(hot_rel_t[t], back), t)

    partner = me + 1 - 2 * core
    mine = pl.multiple_of(core * GROUP, GROUP)
    half = pl.ds(mine, GROUP)
    other_half = pl.ds(pl.multiple_of((1 - core) * GROUP, GROUP), GROUP)

    def along_x(src, dst, sem):
        copies = []
        for i in range(1, XS):
            there = lax.rem(x + i, XS)
            where = {"ent": me + (there - x) * (CORES * ZS)}
            copies.append(remote(src(there), dst, sem.at[0, i], sem.at[1, i], where))
        return copies

    def along_z(src, dst, sem):
        copies = []
        for i in range(1, ZS):
            there = lax.rem(z + i, ZS)
            where = {"ent": me + (there - z) * CORES}
            copies.append(remote(src(there), dst, sem.at[0, i], sem.at[1, i], where))
        return copies

    def along_hist(src, dst, sem):
        copies = []
        for i in range(1, HIST):
            where = {"hist": lax.rem(hist + i, HIST)}
            copies.append(remote(src, dst, sem.at[0, i], sem.at[1, i], where))
        return copies

    def to_core(src, dst, sem, i):
        return remote(src, dst, sem.at[0, i], sem.at[1, i], {"ent": partner})

    def finish(copies):
        for copy in copies:
            copy.wait()

    for t in range(top, -1, -1):
        c = cot[...]
        pre_term = c * coef_pre[t]
        b_send[t] = pack(nn(hot_dst[t], (pre_term * scaling[t]).astype(bf16)))
        exchange(b_send, b_recv, b_sem, t)
        gate_term = c * coef_gate[t]
        gate_low = gate_term.astype(bf16)
        pre_low = pre_term.astype(bf16)
        for j in range(4):
            rows = slice(j * QUART, (j + 1) * QUART)
            piece = nt(gate_low, w_gate[rows, :]) + nt(pre_low, w_self[rows, :])
            part[j] = piece
            part_send[t, j] = piece.astype(bf16)
        for i in range(1, HIST):
            there = lax.rem(hist + i, HIST)
            remote(
                part_send.at[t, there],
                part_recv.at[t, hist],
                part_sem.at[0, t],
                part_sem.at[1, t],
                {"hist": there},
            )
        if t == top:
            forward_messages(t - 1)
        if t > 1:
            forward_messages(t - 2)
        down = jnp.sum(gate_term, axis=0, keepdims=True)
        bias[...] = down if t == top else bias[...] + down
        lows = jnp.concatenate([gate_low, pre_low], axis=1)
        total = jnp.concatenate([tn(states[t, 0], lows), tn(states[t, 1], lows)], axis=0)
        add_grads(grads1, R_GATE, total[:, :QUART], t)
        add_grads(grads1, R_SELF, total[:, QUART:], t)
        if t == 0:
            row = R_QUERY + BIAS_ROW % 8
            grads1[BIAS_ROW // 8, row : row + 1, :] = bias[...]
            core1 = to_core(grads1.at[other_half], core_recv1, core_sem, 0)
        if t < top:
            returned_grads(t + 1)
        if t == 0:
            core1.wait()
            both = (grads1[half] + core_recv1[...]).reshape(ZS, XS, ROWS1, QUART)
            sum1[...] = both
            for xx in range(XS):
                x_send1[xx] = both[:, xx].astype(bf16)
            x1 = along_x(lambda there: x_send1.at[there], x_recv1.at[x], x1_sem)

        if 0 < t < top:
            forward_rest(t - 1)
        wait_bytes(b_recv.at[t, others], b_sem.at[1, t])
        high, low = split(nn(hot_src_t[t], unpack(b_recv[t])))
        sum_send[t] = high
        remote(
            sum_send.at[t], sum_recv.at[t], sum_sem.at[0, t], sum_sem.at[1, t], {"hist": mate}
        )
        near_part = nt(high, w_own[...]) + nt(low, w_own[...]) + c * keep[t] + part[hist]
        if t == top:
            forward_rest(t - 1)
        if t == 0:
            returned_grads(0)
            core2 = to_core(grads2.at[other_half], core_recv2, core_sem, 1)
            finish(x1)
            total = sum1[:, x]
            for i in range(1, XS):
                total = total + x_recv1[lax.rem(x + i, XS)].astype(f32)
            z_send1[...] = total
            z1 = along_z(lambda there: z_send1.at[there], z_recv1.at[z], z1_sem)
        wait_bytes(part_recv.at[t, pl.ds(0, HIST - 1)], part_sem.at[1, t])
        for i in range(1, HIST):
            near_part = near_part + part_recv[t, lax.rem(hist + i, HIST)].astype(f32)
        wait_bytes(sum_recv.at[t], sum_sem.at[1, t])
        c = near_part + nt(sum_recv[t], w_other[...])
        cot[...] = c
        res_send[t] = c.astype(bf16)

        @pl.when(hist == t)
        def _():
            result[t] = res_send[t]

        @pl.when(hist != t)
        def _():
            remote(
                res_send.at[t],
                result.at[hist],
                res_sem.at[0],
                res_sem.at[1],
                {"hist": t},
            )

    core2.wait()
    both = (grads2[half] + core_recv2[...]).reshape(XS, ZS, ROWS2, QUART)
    sum2[...] = both
    x_send2[...] = both.astype(bf16)
    x2 = along_x(lambda there: x_send2.at[there], x_recv2.at[x], x2_sem)

    finish(z1)
    shard1 = z_send1[z]
    for i in range(1, ZS):
        shard1 = shard1 + z_recv1[lax.rem(z + i, ZS)]
    place1 = mine + z * XS + x
    gathered1[hist, place1] = shard1[:KEPT, :].astype(bf16)
    own1 = gathered1.at[hist, place1]
    gx1 = along_x(lambda there: own1, own1, gx1_sem)

    finish(x2)
    total = sum2[x]
    for i in range(1, XS):
        total = total + x_recv2[lax.rem(x + i, XS)].astype(f32)
    z_send2[...] = total
    z2 = along_z(lambda there: z_send2.at[there], z_recv2.at[z], z2_sem)

    finish(gx1)
    line1 = gathered1.at[hist, pl.ds(mine + z * XS, XS)]
    gz1 = along_z(lambda there: line1, line1, gz1_sem)

    finish(z2)
    shard2 = z_send2[z]
    for i in range(1, ZS):
        shard2 = shard2 + z_recv2[lax.rem(z + i, ZS)]
    y_recv2[hist] = jnp.concatenate([shard2[R_REL:, :], shard1[R_QUERY:, :]], axis=0)
    y2 = along_hist(y_recv2.at[hist], y_recv2.at[hist], y2_sem)
    gathered3[hist, place1] = shard2[:R_REL, :].astype(bf16)
    own3 = gathered3.at[hist, place1]
    gx3 = along_x(lambda there: own3, own3, gx3_sem)

    finish(gz1)
    plane1 = gathered1.at[hist, half]
    last = [to_core(plane1, plane1, gc1_sem, 0)]
    gy1 = along_hist(plane1, plane1, gy1_sem)

    finish(y2)
    place2 = mine + x * ZS + z
    for b in range(2):
        wide = jnp.concatenate([y_recv2[2 * b, :8, :], y_recv2[2 * b + 1, :8, :]], axis=1)
        high = wide.astype(bf16).astype(f32)
        twice = nt(jnp.concatenate([high, wide - high], axis=0).astype(bf16), w_neigh[b])
        by_rel = twice[:8, :] + twice[8:, :]
        for j in range(2):
            h = 2 * b + j
            rel_rows = by_rel[:, j * QUART : (j + 1) * QUART] + y_recv2[h, 8:, :]
            gathered2[place2, h] = rel_rows.astype(bf16)
    own2 = gathered2.at[place2]
    gz2 = along_z(lambda there: own2, own2, gz2_sem)
    finish(gx3)
    line3 = gathered3.at[hist, pl.ds(mine + z * XS, XS)]
    gz3 = along_z(lambda there: line3, line3, gz3_sem)
    finish(gz2)
    line2 = gathered2.at[pl.ds(mine + x * ZS, ZS)]
    gx2 = along_x(lambda there: line2, line2, gx2_sem)
    last.append(to_core(line2, line2, gc2_sem, 0))
    finish(gz3)
    plane3 = gathered3.at[hist, half]
    gy3 = along_hist(plane3, plane3, gy3_sem)
    last.append(to_core(plane3, plane3, gc3_sem, 0))
    for i in range(1, HIST):
        gy1[i - 1].wait()
        came = gathered1.at[lax.rem(hist + HIST - i, HIST), half]
        last.append(to_core(came, came, gc1_sem, i))
    for i in range(1, XS):
        gx2[i - 1].wait()
        came = gathered2.at[pl.ds(mine + lax.rem(x + XS - i, XS) * ZS, ZS)]
        last.append(to_core(came, came, gc2_sem, i))
    for i in range(1, HIST):
        gy3[i - 1].wait()
        came = gathered3.at[lax.rem(hist + HIST - i, HIST), half]
        last.append(to_core(came, came, gc3_sem, i))
    finish(last)

    three = pl.ds(0, HIST - 1)
    wait_bytes(result.at[three], res_sem.at[1])
    wait_bytes(res_send.at[three], res_sem.at[0])
    wait_bytes(id_send.at[others], id_sem.at[0])
    wait_bytes(id_recv.at[three], fwd_id_sem.at[0, hist])
    wait_bytes(ids.at[three], ids_sem.at[0, hist])
    wait_bytes(states.at[three], st_sem.at[0, hist])
    for t in range(HIST):
        wait_bytes(f_send.at[t, others], f_sem.at[0, t])
        wait_bytes(b_send.at[t, others], b_sem.at[0, t])
        wait_bytes(part_send.at[t, three], part_sem.at[0, t])
        wait_bytes(sum_send.at[t], sum_sem.at[0, t])


def unfold(
    factor,
    gathered1_in,
    gathered2_in,
    gathered3_in,
    result_in,
    out_states,
    out_neigh,
    out_self,
    out_gate,
    out_bias,
    out_rel,
    gathered1,
    gathered2,
    gathered3,
    result,
    new_states,
    new_neigh,
    new_self,
    new_gate,
    new_bias,
    new_rel,
    in_sem,
    out_sem,
):
    fetched = []
    for src, dst in (
        (gathered1_in, gathered1),
        (result_in, result),
        (gathered2_in, gathered2),
        (gathered3_in, gathered3),
    ):
        fetched.append(pltpu.make_async_copy(src, dst, in_sem.at[len(fetched)]))
        fetched[-1].start()
    stored = []

    def store(src, dst):
        stored.append(pltpu.make_async_copy(src, dst, out_sem.at[len(stored)]))
        stored[-1].start()

    fetched[0].wait()
    for at, new, out in ((R_GATE, new_gate, out_gate), (R_SELF, new_self, out_self)):
        for h in range(HIST):
            rows = gathered1[h].astype(f32)[:, at : at + 8, :] * factor
            new[:, h * QUART : (h + 1) * QUART] = rows.reshape(D, QUART)
        store(new, out)
    fetched[1].wait()
    for h in range(HIST):
        new_states[0, :, h * QUART : (h + 1) * QUART] = result[h].astype(f32)
    store(new_states, out_states)
    fetched[2].wait()
    for h in range(HIST):
        lanes = slice(h * QUART, (h + 1) * QUART)
        by_rel = (gathered2[:, h].astype(f32) * factor).reshape(REL_PAD, QUART)
        new_rel[:, lanes] = by_rel[:NREL, :]
        new_bias[:, lanes] = by_rel[BIAS_ROW : BIAS_ROW + 1, :]
    store(new_rel, out_rel)
    fetched[3].wait()
    for h in range(HIST):
        lanes = slice((h % 2) * QUART, (h % 2 + 1) * QUART)
        rows = gathered3[h, :GROUP].astype(f32) * factor
        for g in range(GROUP):
            at = g % ZS * XS + g // ZS
            new_neigh[h // 2, g * 8 : (g + 1) * 8, lanes] = rows[at]
    store(new_neigh, out_neigh)
    store(new_bias, out_bias)
    for copy in stored:
        copy.wait()


def on_device(
    states,
    w_neigh,
    w_self,
    w_gate,
    b_gate,
    relation,
    edge_src,
    edge_rel,
    edge_dst,
    send_counts,
    query_ent,
    query_rel,
    query_grad,
):
    factor = 1.0 / math.sqrt(HIST * ENT * ROWS)
    vmem = pl.BlockSpec(memory_space=pltpu.VMEM)
    anywhere = pl.BlockSpec(memory_space=pl.ANY)
    dma = pltpu.SemaphoreType.DMA
    shape = jax.ShapeDtypeStruct
    v = pltpu.VMEM
    i32 = jnp.int32
    gathered1, gathered2, gathered3, result = pl.pallas_call(
        kernel,
        out_shape=(
            shape((HIST, ENT, KEPT, QUART), bf16),
            shape((ENT, HIST, 8, QUART), bf16),
            shape((HIST, ENT, 8, QUART), bf16),
            shape((HIST, ROWS, QUART), bf16),
        ),
        in_specs=[anywhere] * 13,
        out_specs=(vmem,) * 4,
        scratch_shapes=[
            v((HIST, 2, ROWS, HALF), bf16),
            v((HALF, QUART), bf16),
            v((QUART, QUART), bf16),
            v((QUART, QUART), bf16),
            v((D, QUART), bf16),
            v((D, QUART), bf16),
            v((1, QUART), f32),
            v((NREL, D), bf16),
            v((HIST, 8, SLOTS), i32),
            v((1, SLOTS), i32),
            v((1, ENT), i32),
            v((1, 128), i32),
            v((1, 128), i32),
            v((128, QUART), f32),
            v((ENT, 128), f32),
            v((HIST, ENT, 128), f32),
            v((REL_PAD, HALF), bf16),
            v((HIST, SLOTS, HALF), bf16),
            v((HIST, ROWS, SLOTS), bf16),
            v((HIST, REL_PAD, SLOTS), bf16),
            v((HIST, SLOTS, ROWS), bf16),
            v((HIST, ENT, 8, QUART), bf16),
            v((HIST, ENT, 8, QUART), bf16),
            v((HIST, ENT, 8, QUART), bf16),
            v((HIST, ENT, 8, QUART), bf16),
            v((ROWS, QUART), f32),
            v((HIST, ROWS, QUART), f32),
            v((HIST, ROWS, QUART), f32),
            v((HIST, ROWS, QUART), f32),
            v((HIST, ROWS, QUART), f32),
            v((1, QUART), f32),
            v((HIST, ROWS, QUART), f32),
            v((HIST, HIST, ROWS, QUART), bf16),
            v((HIST, HIST, ROWS, QUART), bf16),
            v((HIST, ROWS, QUART), bf16),
            v((HIST, ROWS, QUART), bf16),
            v((HIST, ROWS, QUART), bf16),
            v((2, HALF, HALF), bf16),
            v((ENT, ROWS1, QUART), f32),
            v((GROUP, ROWS1, QUART), f32),
            v((ZS, XS, ROWS1, QUART), f32),
            v((XS, ZS, ROWS1, QUART), bf16),
            v((XS, ZS, ROWS1, QUART), bf16),
            v((ZS, ROWS1, QUART), f32),
            v((ZS, ROWS1, QUART), f32),
            v((ENT, ROWS2, QUART), f32),
            v((GROUP, ROWS2, QUART), f32),
            v((XS, ZS, ROWS2, QUART), f32),
            v((XS, ZS, ROWS2, QUART), bf16),
            v((XS, ZS, ROWS2, QUART), bf16),
            v((ZS, ROWS2, QUART), f32),
            v((ZS, ROWS2, QUART), f32),
            v((HIST, 16, QUART), f32),
            dma((17,)),
            dma((2,)),
            dma((2, HIST)),
            dma((3, HIST)),
            dma((2, HIST)),
            dma((2, HIST)),
            dma((2, HIST)),
            dma((2, HIST)),
            dma((2, HIST)),
            dma((2,)),
            dma((2, 2)),
            dma((2, XS)),
            dma((2, ZS)),
            dma((2, XS)),
            dma((2, ZS)),
            dma((2, HIST)),
            dma((2, XS)),
            dma((2, ZS)),
            dma((2, HIST)),
            dma((2, HIST)),
            dma((2, ZS)),
            dma((2, XS)),
            dma((2, XS)),
            dma((2, XS)),
            dma((2, ZS)),
            dma((2, HIST)),
            dma((2, HIST)),
        ],
        compiler_params=pltpu.CompilerParams(
            collective_id=0, has_side_effects=True, vmem_limit_bytes=54 << 20
        ),
        name="encoder_backward",
    )(
        states,
        w_neigh,
        w_self,
        w_gate,
        b_gate.reshape(1, D),
        relation,
        edge_src,
        edge_rel,
        edge_dst,
        send_counts,
        query_ent.reshape(1, 128),
        query_rel.reshape(1, 128),
        query_grad,
    )
    result, grad_neigh, grad_self, grad_gate, grad_bias, grad_rel = pl.pallas_call(
        functools.partial(unfold, factor),
        out_shape=(
            shape((1, ROWS, D), f32),
            shape((2, HALF, HALF), f32),
            shape((D, D), f32),
            shape((D, D), f32),
            shape((1, D), f32),
            shape((NREL, D), f32),
        ),
        in_specs=[anywhere] * 4,
        out_specs=(anywhere,) * 6,
        scratch_shapes=[
            v((HIST, ENT, KEPT, QUART), bf16),
            v((ENT, HIST, 8, QUART), bf16),
            v((HIST, ENT, 8, QUART), bf16),
            v((HIST, ROWS, QUART), bf16),
            v((1, ROWS, D), f32),
            v((2, HALF, HALF), f32),
            v((D, D), f32),
            v((D, D), f32),
            v((1, D), f32),
            v((NREL, D), f32),
            dma((4,)),
            dma((6,)),
        ],
        compiler_params=pltpu.CompilerParams(vmem_limit_bytes=54 << 20),
        name="unfold",
    )(gathered1, gathered2, gathered3, result)
    return result, grad_neigh, grad_self, grad_gate, grad_bias.reshape(D), grad_rel


def solution(mesh):
    return jax.shard_map(
        on_device,
        mesh=mesh,
        in_specs=(
            P("hist", "ent", None),
            P(),
            P(),
            P(),
            P(),
            P(),
            P("hist", "ent"),
            P("hist", "ent"),
            P("hist", "ent"),
            P("hist", "ent"),
            P("ent"),
            P("ent"),
            P("ent", None),
        ),
        out_specs=(P("hist", "ent", None), P(), P(), P(), P(), P()),
        check_vma=False,
    )
```

```python
import functools
import math

import jax
import jax.numpy as jnp
from jax import lax
from jax.experimental import pallas as pl
from jax.experimental.pallas import tpu as pltpu
from jax.sharding import PartitionSpec as P

MESH = pl.DeviceIdType.MESH
bf16 = jnp.bfloat16
f32 = jnp.float32

HIST = 4
ENT = 64
CORES, XS, ZS = 2, 4, 8
ROWS = 256
D = 512
HALF = 256
QUART = 128
SLOTS = 512
NREL = 460
REL_PAD = 512
R_GATE, R_SELF, R_QUERY, ROWS1 = 0, 8, 16, 24
R_NEIGH, R_REL, ROWS2 = 0, 8, 16
KEPT = 16
BIAS_ROW = 508
GROUP = ENT // CORES


def nn(a, b):
    return jnp.dot(a, b, preferred_element_type=f32)


def nt(a, b):
    return lax.dot_general(a, b, (((1,), (1,)), ((), ())), preferred_element_type=f32)


def tn(a, b):
    return lax.dot_general(a, b, (((0,), (0,)), ((), ())), preferred_element_type=f32)


def iota(shape, dim):
    return lax.broadcasted_iota(jnp.int32, shape, dim)


def hot(cond):
    return jnp.where(cond, 1.0, 0.0).astype(bf16)


def split(v):
    high = v.astype(bf16)
    return high, (v - high.astype(f32)).astype(bf16)


def split3(v):
    high = v.astype(bf16)
    middle, low = split(v - high.astype(f32))
    return high, middle, low


def by_shard(v):
    return v.reshape(-1, 8, QUART)


def pack(m):
    return m.reshape(ENT, 8, QUART).astype(bf16)


def unpack(r):
    return r.astype(f32).reshape(SLOTS, QUART).astype(bf16)


def kernel(
    states_in,
    w_neigh_in,
    w_self_in,
    w_gate_in,
    b_gate_in,
    relation_in,
    edge_src_in,
    edge_rel_in,
    edge_dst_in,
    counts_in,
    query_ent_in,
    query_rel_in,
    query_grad_in,
    gathered1,
    gathered2,
    gathered3,
    result,
    states,
    w_cols,
    w_own,
    w_other,
    w_self,
    w_gate,
    b_gate,
    relation,
    ids,
    edge_dst,
    counts,
    query_ent,
    query_rel,
    query_grad,
    id_send,
    id_recv,
    rel_block,
    inputs,
    hot_src_t,
    hot_rel_t,
    hot_dst,
    f_send,
    f_recv,
    b_send,
    b_recv,
    cot,
    keep,
    coef_gate,
    coef_pre,
    scaling,
    bias,
    part,
    part_send,
    part_recv,
    sum_send,
    sum_recv,
    res_send,
    w_neigh,
    grads1,
    core_recv1,
    sum1,
    x_send1,
    x_recv1,
    z_send1,
    z_recv1,
    grads2,
    core_recv2,
    sum2,
    x_send2,
    x_recv2,
    z_send2,
    z_recv2,
    y_recv2,
    fetch_sem,
    id_sem,
    fwd_id_sem,
    st_sem,
    ids_sem,
    f_sem,
    b_sem,
    part_sem,
    sum_sem,
    res_sem,
    core_sem,
    x1_sem,
    z1_sem,
    x2_sem,
    z2_sem,
    y2_sem,
    gx1_sem,
    gz1_sem,
    gy1_sem,
    gc1_sem,
    gz2_sem,
    gx2_sem,
    gc2_sem,
    gx3_sem,
    gz3_sem,
    gy3_sem,
    gc3_sem,
):
    hist = lax.axis_index("hist")
    me = lax.axis_index("ent")
    core = lax.rem(me, CORES)
    z = lax.rem(me // CORES, ZS)
    x = me // (CORES * ZS)
    block = hist // 2
    side = lax.rem(hist, 2)
    mate = hist + 1 - 2 * side

    top = HIST - 1
    barrier = pltpu.get_barrier_semaphore()

    def greet(i, carry):
        pl.semaphore_signal(
            barrier, inc=1, device_id={"ent": lax.rem(me + i, ENT)}, device_id_type=MESH
        )
        return carry

    lax.fori_loop(1, ENT, greet, 0)
    for i in range(1, HIST):
        pl.semaphore_signal(
            barrier, inc=1, device_id={"hist": lax.rem(hist + i, HIST)}, device_id_type=MESH
        )

    cols = pl.ds(pl.multiple_of(hist * QUART, QUART), QUART)
    near = pl.ds(pl.multiple_of(side * QUART, QUART), QUART)
    far = pl.ds(pl.multiple_of((1 - side) * QUART, QUART), QUART)
    fetched = []

    def fetch(src, dst):
        copy = pltpu.make_async_copy(src, dst, fetch_sem.at[len(fetched)])
        copy.start()
        fetched.append(copy)

    fetch(edge_dst_in, edge_dst)
    fetch(counts_in, counts)
    fetch(edge_src_in, ids.at[hist, pl.ds(0, 1)])
    fetch(edge_rel_in, ids.at[hist, pl.ds(1, 1)])
    fetch(states_in.at[0, :, pl.ds(0, HALF)], states.at[hist, 0])
    fetch(states_in.at[0, :, pl.ds(HALF, HALF)], states.at[hist, 1])
    fetch(relation_in, relation)
    fetch(w_neigh_in.at[block, :, near], w_cols)
    fetch(w_neigh_in.at[block, near, near], w_own)
    fetch(w_neigh_in.at[block, near, far], w_other)
    fetch(w_self_in.at[:, cols], w_self)
    fetch(w_gate_in.at[:, cols], w_gate)
    fetch(b_gate_in.at[:, cols], b_gate)
    fetch(query_ent_in, query_ent)
    fetch(query_rel_in, query_rel)
    fetch(query_grad_in.at[:, cols], query_grad)
    fetch(w_neigh_in, w_neigh)

    fetched[0].wait()
    fetched[1].wait()
    dst = edge_dst[...].astype(f32)
    own_slot = jnp.where((iota((ENT, SLOTS), 1) >> 3) == iota((ENT, SLOTS), 0), dst, 0.0)
    to_lane = hot((iota((SLOTS, 128), 0) & 7) == iota((SLOTS, 128), 1))
    target = nn(own_slot.astype(bf16), to_lane)
    own_count = jnp.where(
        iota((ENT, ENT), 0) == iota((ENT, ENT), 1), counts[...].astype(f32), 0.0
    )
    limit = nn(own_count.astype(bf16), jnp.ones((ENT, 128), bf16))
    id_send[...] = jnp.where(iota((ENT, 128), 1).astype(f32) < limit, target, -1.0)

    for i in range(2, 6):
        fetched[i].wait()

    def wait_bytes(ref, sem):
        pltpu.make_async_copy(ref, ref, sem).wait()

    def remote(src, dst, send, recv, where):
        copy = pltpu.make_async_remote_copy(
            src_ref=src,
            dst_ref=dst,
            send_sem=send,
            recv_sem=recv,
            device_id=where,
            device_id_type=MESH,
        )
        copy.start()
        return copy

    def share_states(t):
        @pl.when(hist == t)
        def _():
            order = [(t + 3) % HIST, (t + 1) % HIST, (t + 2) % HIST]
            for p in order:
                remote(
                    ids.at[t], ids.at[t], ids_sem.at[0, t], ids_sem.at[1, t], {"hist": p}
                )
            for first in (True, False):
                for p in order:
                    b = p // 2 if first else 1 - p // 2
                    remote(
                        states.at[t, b],
                        states.at[t, b],
                        st_sem.at[0, t],
                        st_sem.at[1 + b, t],
                        {"hist": p},
                    )

    pl.semaphore_wait(barrier, ENT - 1 + HIST - 1)
    share_states(HIST - 1)

    def send_ids(i, carry):
        peer = lax.rem(me + i, ENT)
        remote(
            id_send.at[pl.ds(peer, 1)],
            id_recv.at[hist, pl.ds(me, 1)],
            id_sem.at[0],
            id_sem.at[1],
            {"ent": peer},
        )
        return carry

    lax.fori_loop(1, ENT, send_ids, 0)
    id_recv[hist, pl.ds(me, 1), :] = id_send[pl.ds(me, 1), :]

    def exchange(send, recv, sem, t):
        def step(i, carry):
            peer = lax.rem(me + i, ENT)
            remote(send.at[t, peer], recv.at[t, me], sem.at[0, t], sem.at[1, t], {"ent": peer})
            return carry

        lax.fori_loop(1, ENT, step, 0)
        recv[t, me] = send[t, me]

    others = pl.ds(0, ENT - 1)

    for i in range(6, len(fetched)):
        fetched[i].wait()
    rel_block[NREL // 16 * 16 :, :] = jnp.zeros((REL_PAD - NREL // 16 * 16, HALF), bf16)
    rel_block[:NREL, :] = relation[:, pl.ds(pl.multiple_of(block * HALF, HALF), HALF)]

    q_parts = split3(query_grad[...])
    hot_query = hot(iota((ROWS, 128), 0) == query_ent[...])
    cot[...] = nn(hot_query, q_parts[0]) + (nn(hot_query, q_parts[1]) + nn(hot_query, q_parts[2]))
    hot_query = hot(iota((REL_PAD, 128), 0) == query_rel[...])
    by_query = nn(hot_query, q_parts[0]) + (nn(hot_query, q_parts[1]) + nn(hot_query, q_parts[2]))
    for g in range(ENT):
        c, xx, zz = g // GROUP, g // ZS % XS, g % ZS
        at = c * GROUP + zz * XS + xx
        grads1[at, R_QUERY : R_QUERY + 8, :] = by_query[g * 8 : (g + 1) * 8, :]
    grads2[GROUP:, R_NEIGH : R_NEIGH + 8, :] = jnp.zeros((GROUP, 8, QUART), f32)

    def forward_messages(t):
        @pl.when(hist != t)
        def _():
            wait_bytes(ids.at[t], ids_sem.at[1, t])
            wait_bytes(states.at[t, block], st_sem.at[1 + block, t])

        if t == top:
            for later in range(t - 1, -1, -1):
                share_states(later)
        hot_src_t[t] = hot(iota((ROWS, SLOTS), 0) == ids[t, 0:1, :])
        hot_rel_t[t] = hot(iota((REL_PAD, SLOTS), 0) == ids[t, 1:2, :])
        inputs[t] = (
            tn(hot_src_t[t], states[t, block]) + tn(hot_rel_t[t], rel_block[...])
        ).astype(bf16)
        f_send[t] = pack(nn(inputs[t], w_cols[...]))
        exchange(f_send, f_recv, f_sem, t)

    def forward_rest(t):
        @pl.when(hist != t)
        def _():
            wait_bytes(states.at[t, 1 - block], st_sem.at[2 - block, t])

        logit = nn(states[t, 0], w_gate[:HALF, :]) + nn(states[t, 1], w_gate[HALF:, :])
        dense = nn(states[t, 0], w_self[:HALF, :]) + nn(states[t, 1], w_self[HALF:, :])
        opened = jax.nn.sigmoid(logit + b_gate[...])
        shut = 1.0 - opened

        @pl.when(hist != t)
        def _():
            wait_bytes(id_recv.at[t], fwd_id_sem.at[1, t])

        to_slot = hot((iota((SLOTS, ENT), 0) >> 3) == iota((SLOTS, ENT), 1))
        arrived = nn(to_slot, id_recv[t].astype(bf16))
        arrived = jnp.where(
            iota((SLOTS, 128), 1) == (iota((SLOTS, 128), 0) & 7), arrived, 0.0
        ).astype(bf16)
        ones = jnp.ones((ROWS, 128), bf16)
        hot_dst[t] = hot(nt(arrived, ones) == iota((SLOTS, ROWS), 1).astype(f32))
        hot_dst_t = hot(nt(ones, arrived) == iota((ROWS, SLOTS), 0).astype(f32))
        degree = nn(hot_dst_t, jnp.ones((SLOTS, QUART), bf16))
        scale = 1.0 / jnp.maximum(degree, 1.0)
        scaling[t] = scale
        wait_bytes(f_recv.at[t, others], f_sem.at[1, t])
        pre_act = nn(hot_dst_t, unpack(f_recv[t])) * scale + dense
        sig = jax.nn.sigmoid(pre_act)
        keep[t] = shut
        own = states[t, block, :, near].astype(f32)
        coef_gate[t] = (pre_act * sig - own) * opened * shut
        coef_pre[t] = opened * (sig * (1.0 + pre_act * (1.0 - sig)))

    forward_messages(top)
    wait_bytes(id_recv.at[hist, others], id_sem.at[1])
    for i in range(1, HIST):
        remote(
            id_recv.at[hist],
            id_recv.at[hist],
            fwd_id_sem.at[0, hist],
            fwd_id_sem.at[1, hist],
            {"hist": lax.rem(hist + i, HIST)},
        )
    forward_rest(top)

    def add_grads(ref, at, value, t, owners=ENT):
        if t == top:
            ref[:owners, at : at + 8, :] = by_shard(value)
        else:
            ref[:owners, at : at + 8, :] += by_shard(value)

    def returned_grads(t):
        back = unpack(b_recv[t])
        add_grads(grads2, R_NEIGH, tn(inputs[t], back), t, GROUP)
        add_grads(grads2, R_REL, nn(hot_rel_t[t], back), t)

    partner = me + 1 - 2 * core
    mine = pl.multiple_of(core * GROUP, GROUP)
    half = pl.ds(mine, GROUP)
    other_half = pl.ds(pl.multiple_of((1 - core) * GROUP, GROUP), GROUP)

    def along_x(src, dst, sem):
        copies = []
        for i in range(1, XS):
            there = lax.rem(x + i, XS)
            where = {"ent": me + (there - x) * (CORES * ZS)}
            copies.append(remote(src(there), dst, sem.at[0, i], sem.at[1, i], where))
        return copies

    def along_z(src, dst, sem):
        copies = []
        for i in range(1, ZS):
            there = lax.rem(z + i, ZS)
            where = {"ent": me + (there - z) * CORES}
            copies.append(remote(src(there), dst, sem.at[0, i], sem.at[1, i], where))
        return copies

    def along_hist(src, dst, sem):
        copies = []
        for i in range(1, HIST):
            where = {"hist": lax.rem(hist + i, HIST)}
            copies.append(remote(src, dst, sem.at[0, i], sem.at[1, i], where))
        return copies

    def to_core(src, dst, sem, i):
        return remote(src, dst, sem.at[0, i], sem.at[1, i], {"ent": partner})

    def finish(copies):
        for copy in copies:
            copy.wait()

    def send_result(t):
        @pl.when(hist != t)
        def _():
            remote(
                res_send.at[t],
                result.at[hist],
                res_sem.at[0],
                res_sem.at[1],
                {"hist": t},
            )

    for t in range(top, -1, -1):
        c = cot[...]
        pre_term = c * coef_pre[t]
        b_send[t] = pack(nn(hot_dst[t], (pre_term * scaling[t]).astype(bf16)))
        exchange(b_send, b_recv, b_sem, t)
        gate_term = c * coef_gate[t]
        gate_low = gate_term.astype(bf16)
        pre_low = pre_term.astype(bf16)
        for j in range(4):
            rows = slice(j * QUART, (j + 1) * QUART)
            piece = nt(gate_low, w_gate[rows, :]) + nt(pre_low, w_self[rows, :])
            part[j] = piece
            part_send[t, j] = piece.astype(bf16)
        for i in range(1, HIST):
            there = lax.rem(hist + i, HIST)
            remote(
                part_send.at[t, there],
                part_recv.at[t, hist],
                part_sem.at[0, t],
                part_sem.at[1, t],
                {"hist": there},
            )
        if t == top:
            forward_messages(t - 1)
        if t > 1:
            forward_messages(t - 2)
        down = jnp.sum(gate_term, axis=0, keepdims=True)
        bias[...] = down if t == top else bias[...] + down
        lows = jnp.concatenate([gate_low, pre_low], axis=1)
        total = jnp.concatenate([tn(states[t, 0], lows), tn(states[t, 1], lows)], axis=0)
        add_grads(grads1, R_GATE, total[:, :QUART], t)
        add_grads(grads1, R_SELF, total[:, QUART:], t)
        if t == 0:
            row = R_QUERY + BIAS_ROW % 8
            grads1[BIAS_ROW // 8, row : row + 1, :] = bias[...]
            core1 = to_core(grads1.at[other_half], core_recv1, core_sem, 0)
        if t < top:
            returned_grads(t + 1)
        if t == 0:
            core1.wait()
            both = (grads1[half] + core_recv1[...]).reshape(ZS, XS, ROWS1, QUART)
            sum1[...] = both
            for xx in range(XS):
                x_send1[xx] = both[:, xx].astype(bf16)
            x1 = along_x(lambda there: x_send1.at[there], x_recv1.at[x], x1_sem)

        if 0 < t < top:
            forward_rest(t - 1)
        wait_bytes(b_recv.at[t, others], b_sem.at[1, t])
        high, low = split(nn(hot_src_t[t], unpack(b_recv[t])))
        sum_send[t] = high
        remote(
            sum_send.at[t], sum_recv.at[t], sum_sem.at[0, t], sum_sem.at[1, t], {"hist": mate}
        )
        if t < top:
            send_result(t + 1)
        near_part = nt(high, w_own[...]) + nt(low, w_own[...]) + c * keep[t] + part[hist]
        if t == top:
            forward_rest(t - 1)
        if t == 0:
            returned_grads(0)
            core2 = to_core(grads2.at[other_half], core_recv2, core_sem, 1)
            finish(x1)
            total = sum1[:, x]
            for i in range(1, XS):
                total = total + x_recv1[lax.rem(x + i, XS)].astype(f32)
            z_send1[...] = total
            z1 = along_z(lambda there: z_send1.at[there], z_recv1.at[z], z1_sem)
        wait_bytes(part_recv.at[t, pl.ds(0, HIST - 1)], part_sem.at[1, t])
        for i in range(1, HIST):
            near_part = near_part + part_recv[t, lax.rem(hist + i, HIST)].astype(f32)
        wait_bytes(sum_recv.at[t], sum_sem.at[1, t])
        c = near_part + nt(sum_recv[t], w_other[...])
        cot[...] = c
        res_send[t] = c.astype(bf16)

        @pl.when(hist == t)
        def _():
            result[t] = res_send[t]

        if t == 0:
            send_result(t)

    core2.wait()
    both = (grads2[half] + core_recv2[...]).reshape(XS, ZS, ROWS2, QUART)
    sum2[...] = both
    x_send2[...] = both.astype(bf16)
    x2 = along_x(lambda there: x_send2.at[there], x_recv2.at[x], x2_sem)

    finish(z1)
    shard1 = z_send1[z]
    for i in range(1, ZS):
        shard1 = shard1 + z_recv1[lax.rem(z + i, ZS)]
    place1 = mine + z * XS + x
    gathered1[hist, place1] = shard1[:KEPT, :].astype(bf16)
    own1 = gathered1.at[hist, place1]
    gx1 = along_x(lambda there: own1, own1, gx1_sem)

    finish(x2)
    total = sum2[x]
    for i in range(1, XS):
        total = total + x_recv2[lax.rem(x + i, XS)].astype(f32)
    z_send2[...] = total
    z2 = along_z(lambda there: z_send2.at[there], z_recv2.at[z], z2_sem)

    finish(gx1)
    line1 = gathered1.at[hist, pl.ds(mine + z * XS, XS)]
    gz1 = along_z(lambda there: line1, line1, gz1_sem)

    finish(z2)
    shard2 = z_send2[z]
    for i in range(1, ZS):
        shard2 = shard2 + z_recv2[lax.rem(z + i, ZS)]
    y_recv2[hist] = jnp.concatenate([shard2[R_REL:, :], shard1[R_QUERY:, :]], axis=0)
    y2 = along_hist(y_recv2.at[hist], y_recv2.at[hist], y2_sem)
    gathered3[hist, place1] = shard2[:R_REL, :].astype(bf16)
    own3 = gathered3.at[hist, place1]
    gx3 = along_x(lambda there: own3, own3, gx3_sem)

    finish(gz1)
    plane1 = gathered1.at[hist, half]
    last = [to_core(plane1, plane1, gc1_sem, 0)]
    gy1 = along_hist(plane1, plane1, gy1_sem)

    finish(y2)
    place2 = mine + x * ZS + z
    for b in range(2):
        wide = jnp.concatenate([y_recv2[2 * b, :8, :], y_recv2[2 * b + 1, :8, :]], axis=1)
        high = wide.astype(bf16).astype(f32)
        twice = nt(jnp.concatenate([high, wide - high], axis=0).astype(bf16), w_neigh[b])
        by_rel = twice[:8, :] + twice[8:, :]
        for j in range(2):
            h = 2 * b + j
            rel_rows = by_rel[:, j * QUART : (j + 1) * QUART] + y_recv2[h, 8:, :]
            gathered2[place2, h] = rel_rows.astype(bf16)
    own2 = gathered2.at[place2]
    gz2 = along_z(lambda there: own2, own2, gz2_sem)
    finish(gx3)
    line3 = gathered3.at[hist, pl.ds(mine + z * XS, XS)]
    gz3 = along_z(lambda there: line3, line3, gz3_sem)
    finish(gz2)
    line2 = gathered2.at[pl.ds(mine + x * ZS, ZS)]
    gx2 = along_x(lambda there: line2, line2, gx2_sem)
    last.append(to_core(line2, line2, gc2_sem, 0))
    finish(gz3)
    plane3 = gathered3.at[hist, half]
    gy3 = along_hist(plane3, plane3, gy3_sem)
    last.append(to_core(plane3, plane3, gc3_sem, 0))
    for i in range(1, HIST):
        gy1[i - 1].wait()
        came = gathered1.at[lax.rem(hist + HIST - i, HIST), half]
        last.append(to_core(came, came, gc1_sem, i))
    for i in range(1, XS):
        gx2[i - 1].wait()
        came = gathered2.at[pl.ds(mine + lax.rem(x + XS - i, XS) * ZS, ZS)]
        last.append(to_core(came, came, gc2_sem, i))
    for i in range(1, HIST):
        gy3[i - 1].wait()
        came = gathered3.at[lax.rem(hist + HIST - i, HIST), half]
        last.append(to_core(came, came, gc3_sem, i))
    finish(last)

    three = pl.ds(0, HIST - 1)
    wait_bytes(result.at[three], res_sem.at[1])
    wait_bytes(res_send.at[three], res_sem.at[0])
    wait_bytes(id_send.at[others], id_sem.at[0])
    wait_bytes(id_recv.at[three], fwd_id_sem.at[0, hist])
    wait_bytes(ids.at[three], ids_sem.at[0, hist])
    wait_bytes(states.at[three], st_sem.at[0, hist])
    for t in range(HIST):
        wait_bytes(f_send.at[t, others], f_sem.at[0, t])
        wait_bytes(b_send.at[t, others], b_sem.at[0, t])
        wait_bytes(part_send.at[t, three], part_sem.at[0, t])
        wait_bytes(sum_send.at[t], sum_sem.at[0, t])


def unfold(
    factor,
    gathered1_in,
    gathered2_in,
    gathered3_in,
    result_in,
    out_states,
    out_neigh,
    out_self,
    out_gate,
    out_bias,
    out_rel,
    gathered1,
    gathered2,
    gathered3,
    result,
    new_states,
    new_neigh,
    new_self,
    new_gate,
    new_bias,
    new_rel,
    in_sem,
    out_sem,
):
    fetched = []
    for src, dst in (
        (gathered1_in, gathered1),
        (result_in, result),
        (gathered2_in, gathered2),
        (gathered3_in, gathered3),
    ):
        fetched.append(pltpu.make_async_copy(src, dst, in_sem.at[len(fetched)]))
        fetched[-1].start()
    stored = []

    def store(src, dst):
        stored.append(pltpu.make_async_copy(src, dst, out_sem.at[len(stored)]))
        stored[-1].start()

    fetched[0].wait()
    for at, new, out in ((R_GATE, new_gate, out_gate), (R_SELF, new_self, out_self)):
        for h in range(HIST):
            rows = gathered1[h].astype(f32)[:, at : at + 8, :] * factor
            new[:, h * QUART : (h + 1) * QUART] = rows.reshape(D, QUART)
        store(new, out)
    fetched[1].wait()
    for h in range(HIST):
        new_states[0, :, h * QUART : (h + 1) * QUART] = result[h].astype(f32)
    store(new_states, out_states)
    fetched[2].wait()
    for h in range(HIST):
        lanes = slice(h * QUART, (h + 1) * QUART)
        by_rel = (gathered2[:, h].astype(f32) * factor).reshape(REL_PAD, QUART)
        new_rel[:, lanes] = by_rel[:NREL, :]
        new_bias[:, lanes] = by_rel[BIAS_ROW : BIAS_ROW + 1, :]
    store(new_rel, out_rel)
    fetched[3].wait()
    for h in range(HIST):
        lanes = slice((h % 2) * QUART, (h % 2 + 1) * QUART)
        rows = gathered3[h, :GROUP].astype(f32) * factor
        for g in range(GROUP):
            at = g % ZS * XS + g // ZS
            new_neigh[h // 2, g * 8 : (g + 1) * 8, lanes] = rows[at]
    store(new_neigh, out_neigh)
    store(new_bias, out_bias)
    for copy in stored:
        copy.wait()


def on_device(
    states,
    w_neigh,
    w_self,
    w_gate,
    b_gate,
    relation,
    edge_src,
    edge_rel,
    edge_dst,
    send_counts,
    query_ent,
    query_rel,
    query_grad,
):
    factor = 1.0 / math.sqrt(HIST * ENT * ROWS)
    vmem = pl.BlockSpec(memory_space=pltpu.VMEM)
    anywhere = pl.BlockSpec(memory_space=pl.ANY)
    dma = pltpu.SemaphoreType.DMA
    shape = jax.ShapeDtypeStruct
    v = pltpu.VMEM
    i32 = jnp.int32
    gathered1, gathered2, gathered3, result = pl.pallas_call(
        kernel,
        out_shape=(
            shape((HIST, ENT, KEPT, QUART), bf16),
            shape((ENT, HIST, 8, QUART), bf16),
            shape((HIST, ENT, 8, QUART), bf16),
            shape((HIST, ROWS, QUART), bf16),
        ),
        in_specs=[anywhere] * 13,
        out_specs=(vmem,) * 4,
        scratch_shapes=[
            v((HIST, 2, ROWS, HALF), bf16),
            v((HALF, QUART), bf16),
            v((QUART, QUART), bf16),
            v((QUART, QUART), bf16),
            v((D, QUART), bf16),
            v((D, QUART), bf16),
            v((1, QUART), f32),
            v((NREL, D), bf16),
            v((HIST, 8, SLOTS), i32),
            v((1, SLOTS), i32),
            v((1, ENT), i32),
            v((1, 128), i32),
            v((1, 128), i32),
            v((128, QUART), f32),
            v((ENT, 128), f32),
            v((HIST, ENT, 128), f32),
            v((REL_PAD, HALF), bf16),
            v((HIST, SLOTS, HALF), bf16),
            v((HIST, ROWS, SLOTS), bf16),
            v((HIST, REL_PAD, SLOTS), bf16),
            v((HIST, SLOTS, ROWS), bf16),
            v((HIST, ENT, 8, QUART), bf16),
            v((HIST, ENT, 8, QUART), bf16),
            v((HIST, ENT, 8, QUART), bf16),
            v((HIST, ENT, 8, QUART), bf16),
            v((ROWS, QUART), f32),
            v((HIST, ROWS, QUART), f32),
            v((HIST, ROWS, QUART), f32),
            v((HIST, ROWS, QUART), f32),
            v((HIST, ROWS, QUART), f32),
            v((1, QUART), f32),
            v((HIST, ROWS, QUART), f32),
            v((HIST, HIST, ROWS, QUART), bf16),
            v((HIST, HIST, ROWS, QUART), bf16),
            v((HIST, ROWS, QUART), bf16),
            v((HIST, ROWS, QUART), bf16),
            v((HIST, ROWS, QUART), bf16),
            v((2, HALF, HALF), bf16),
            v((ENT, ROWS1, QUART), f32),
            v((GROUP, ROWS1, QUART), f32),
            v((ZS, XS, ROWS1, QUART), f32),
            v((XS, ZS, ROWS1, QUART), bf16),
            v((XS, ZS, ROWS1, QUART), bf16),
            v((ZS, ROWS1, QUART), f32),
            v((ZS, ROWS1, QUART), f32),
            v((ENT, ROWS2, QUART), f32),
            v((GROUP, ROWS2, QUART), f32),
            v((XS, ZS, ROWS2, QUART), f32),
            v((XS, ZS, ROWS2, QUART), bf16),
            v((XS, ZS, ROWS2, QUART), bf16),
            v((ZS, ROWS2, QUART), f32),
            v((ZS, ROWS2, QUART), f32),
            v((HIST, 16, QUART), f32),
            dma((17,)),
            dma((2,)),
            dma((2, HIST)),
            dma((3, HIST)),
            dma((2, HIST)),
            dma((2, HIST)),
            dma((2, HIST)),
            dma((2, HIST)),
            dma((2, HIST)),
            dma((2,)),
            dma((2, 2)),
            dma((2, XS)),
            dma((2, ZS)),
            dma((2, XS)),
            dma((2, ZS)),
            dma((2, HIST)),
            dma((2, XS)),
            dma((2, ZS)),
            dma((2, HIST)),
            dma((2, HIST)),
            dma((2, ZS)),
            dma((2, XS)),
            dma((2, XS)),
            dma((2, XS)),
            dma((2, ZS)),
            dma((2, HIST)),
            dma((2, HIST)),
        ],
        compiler_params=pltpu.CompilerParams(
            collective_id=0, has_side_effects=True, vmem_limit_bytes=54 << 20
        ),
        name="encoder_backward",
    )(
        states,
        w_neigh,
        w_self,
        w_gate,
        b_gate.reshape(1, D),
        relation,
        edge_src,
        edge_rel,
        edge_dst,
        send_counts,
        query_ent.reshape(1, 128),
        query_rel.reshape(1, 128),
        query_grad,
    )
    result, grad_neigh, grad_self, grad_gate, grad_bias, grad_rel = pl.pallas_call(
        functools.partial(unfold, factor),
        out_shape=(
            shape((1, ROWS, D), f32),
            shape((2, HALF, HALF), f32),
            shape((D, D), f32),
            shape((D, D), f32),
            shape((1, D), f32),
            shape((NREL, D), f32),
        ),
        in_specs=[anywhere] * 4,
        out_specs=(anywhere,) * 6,
        scratch_shapes=[
            v((HIST, ENT, KEPT, QUART), bf16),
            v((ENT, HIST, 8, QUART), bf16),
            v((HIST, ENT, 8, QUART), bf16),
            v((HIST, ROWS, QUART), bf16),
            v((1, ROWS, D), f32),
            v((2, HALF, HALF), f32),
            v((D, D), f32),
            v((D, D), f32),
            v((1, D), f32),
            v((NREL, D), f32),
            dma((4,)),
            dma((6,)),
        ],
        compiler_params=pltpu.CompilerParams(vmem_limit_bytes=54 << 20),
        name="unfold",
    )(gathered1, gathered2, gathered3, result)
    return result, grad_neigh, grad_self, grad_gate, grad_bias.reshape(D), grad_rel


def solution(mesh):
    return jax.shard_map(
        on_device,
        mesh=mesh,
        in_specs=(
            P("hist", "ent", None),
            P(),
            P(),
            P(),
            P(),
            P(),
            P("hist", "ent"),
            P("hist", "ent"),
            P("hist", "ent"),
            P("hist", "ent"),
            P("ent"),
            P("ent"),
            P("ent", None),
        ),
        out_specs=(P("hist", "ent", None), P(), P(), P(), P(), P()),
        check_vma=False,
    )
```

```python
import functools
import math

import jax
import jax.numpy as jnp
from jax import lax
from jax.experimental import pallas as pl
from jax.experimental.pallas import tpu as pltpu
from jax.sharding import PartitionSpec as P

MESH = pl.DeviceIdType.MESH
bf16 = jnp.bfloat16
f32 = jnp.float32

HIST = 4
ENT = 64
CORES, XS, ZS = 2, 4, 8
ROWS = 256
D = 512
HALF = 256
QUART = 128
SLOTS = 512
NREL = 460
REL_PAD = 512
R_GATE, R_SELF, R_QUERY, ROWS1 = 0, 8, 16, 24
R_NEIGH, R_REL, ROWS2 = 0, 8, 16
KEPT = 8
BIAS_ROW = 508
GROUP = ENT // CORES


def nn(a, b):
    return jnp.dot(a, b, preferred_element_type=f32)


def nt(a, b):
    return lax.dot_general(a, b, (((1,), (1,)), ((), ())), preferred_element_type=f32)


def tn(a, b):
    return lax.dot_general(a, b, (((0,), (0,)), ((), ())), preferred_element_type=f32)


def iota(shape, dim):
    return lax.broadcasted_iota(jnp.int32, shape, dim)


def hot(cond):
    return jnp.where(cond, 1.0, 0.0).astype(bf16)


def split(v):
    high = v.astype(bf16)
    return high, (v - high.astype(f32)).astype(bf16)


def split3(v):
    high = v.astype(bf16)
    middle, low = split(v - high.astype(f32))
    return high, middle, low


def by_shard(v):
    return v.reshape(-1, 8, QUART)


def pack(m):
    return m.reshape(ENT, 8, QUART).astype(bf16)


def unpack(r):
    return r.astype(f32).reshape(SLOTS, QUART).astype(bf16)


def kernel(
    states_in,
    w_neigh_in,
    w_self_in,
    w_gate_in,
    b_gate_in,
    relation_in,
    edge_src_in,
    edge_rel_in,
    edge_dst_in,
    counts_in,
    query_ent_in,
    query_rel_in,
    query_grad_in,
    gathered1,
    gathered2,
    gathered3,
    gathered4,
    result,
    states,
    w_cols,
    w_own,
    w_other,
    w_self,
    w_gate,
    b_gate,
    relation,
    ids,
    edge_dst,
    counts,
    query_ent,
    query_rel,
    query_grad,
    id_send,
    id_recv,
    rel_block,
    inputs,
    hot_src_t,
    hot_rel_t,
    hot_dst,
    f_send,
    f_recv,
    b_send,
    b_recv,
    cot,
    keep,
    coef_gate,
    coef_pre,
    scaling,
    bias,
    part,
    part_send,
    part_recv,
    sum_send,
    sum_recv,
    res_send,
    w_neigh,
    grads1,
    core_recv1,
    sum1,
    x_send1,
    x_recv1,
    z_send1,
    z_recv1,
    grads2,
    core_recv2,
    sum2,
    x_send2,
    x_recv2,
    z_send2,
    z_recv2,
    y_recv2,
    fetch_sem,
    id_sem,
    fwd_id_sem,
    st_sem,
    ids_sem,
    f_sem,
    b_sem,
    part_sem,
    sum_sem,
    res_sem,
    core_sem,
    x1_sem,
    z1_sem,
    x2_sem,
    z2_sem,
    y2_sem,
    gx1_sem,
    gz1_sem,
    gy1_sem,
    gc1_sem,
    gz2_sem,
    gx2_sem,
    gc2_sem,
    gx3_sem,
    gz3_sem,
    gy3_sem,
    gc3_sem,
    gy4_sem,
    gz4_sem,
    gx4_sem,
    gc4_sem,
):
    hist = lax.axis_index("hist")
    me = lax.axis_index("ent")
    core = lax.rem(me, CORES)
    z = lax.rem(me // CORES, ZS)
    x = me // (CORES * ZS)
    block = hist // 2
    side = lax.rem(hist, 2)
    mate = hist + 1 - 2 * side

    top = HIST - 1
    barrier = pltpu.get_barrier_semaphore()

    def greet(i, carry):
        pl.semaphore_signal(
            barrier, inc=1, device_id={"ent": lax.rem(me + i, ENT)}, device_id_type=MESH
        )
        return carry

    lax.fori_loop(1, ENT, greet, 0)
    for i in range(1, HIST):
        pl.semaphore_signal(
            barrier, inc=1, device_id={"hist": lax.rem(hist + i, HIST)}, device_id_type=MESH
        )

    cols = pl.ds(pl.multiple_of(hist * QUART, QUART), QUART)
    near = pl.ds(pl.multiple_of(side * QUART, QUART), QUART)
    far = pl.ds(pl.multiple_of((1 - side) * QUART, QUART), QUART)
    fetched = []

    def fetch(src, dst):
        copy = pltpu.make_async_copy(src, dst, fetch_sem.at[len(fetched)])
        copy.start()
        fetched.append(copy)

    fetch(edge_dst_in, edge_dst)
    fetch(counts_in, counts)
    fetch(edge_src_in, ids.at[hist, pl.ds(0, 1)])
    fetch(edge_rel_in, ids.at[hist, pl.ds(1, 1)])
    fetch(states_in.at[0, :, pl.ds(0, HALF)], states.at[hist, 0])
    fetch(states_in.at[0, :, pl.ds(HALF, HALF)], states.at[hist, 1])
    fetch(relation_in, relation)
    fetch(w_neigh_in.at[block, :, near], w_cols)
    fetch(w_neigh_in.at[block, near, near], w_own)
    fetch(w_neigh_in.at[block, near, far], w_other)
    fetch(w_self_in.at[:, cols], w_self)
    fetch(w_gate_in.at[:, cols], w_gate)
    fetch(b_gate_in.at[:, cols], b_gate)
    fetch(query_ent_in, query_ent)
    fetch(query_rel_in, query_rel)
    fetch(query_grad_in.at[:, cols], query_grad)
    fetch(w_neigh_in, w_neigh)

    fetched[0].wait()
    fetched[1].wait()
    dst = edge_dst[...].astype(f32)
    own_slot = jnp.where((iota((ENT, SLOTS), 1) >> 3) == iota((ENT, SLOTS), 0), dst, 0.0)
    to_lane = hot((iota((SLOTS, 128), 0) & 7) == iota((SLOTS, 128), 1))
    target = nn(own_slot.astype(bf16), to_lane)
    own_count = jnp.where(
        iota((ENT, ENT), 0) == iota((ENT, ENT), 1), counts[...].astype(f32), 0.0
    )
    limit = nn(own_count.astype(bf16), jnp.ones((ENT, 128), bf16))
    id_send[...] = jnp.where(iota((ENT, 128), 1).astype(f32) < limit, target, -1.0)

    for i in range(2, 6):
        fetched[i].wait()

    def wait_bytes(ref, sem):
        pltpu.make_async_copy(ref, ref, sem).wait()

    def remote(src, dst, send, recv, where):
        copy = pltpu.make_async_remote_copy(
            src_ref=src,
            dst_ref=dst,
            send_sem=send,
            recv_sem=recv,
            device_id=where,
            device_id_type=MESH,
        )
        copy.start()
        return copy

    def share_states(t):
        @pl.when(hist == t)
        def _():
            order = [(t + 3) % HIST, (t + 1) % HIST, (t + 2) % HIST]
            for p in order:
                remote(
                    ids.at[t], ids.at[t], ids_sem.at[0, t], ids_sem.at[1, t], {"hist": p}
                )
            for first in (True, False):
                for p in order:
                    b = p // 2 if first else 1 - p // 2
                    remote(
                        states.at[t, b],
                        states.at[t, b],
                        st_sem.at[0, t],
                        st_sem.at[1 + b, t],
                        {"hist": p},
                    )

    pl.semaphore_wait(barrier, ENT - 1 + HIST - 1)
    share_states(HIST - 1)

    def send_ids(i, carry):
        peer = lax.rem(me + i, ENT)
        remote(
            id_send.at[pl.ds(peer, 1)],
            id_recv.at[hist, pl.ds(me, 1)],
            id_sem.at[0],
            id_sem.at[1],
            {"ent": peer},
        )
        return carry

    lax.fori_loop(1, ENT, send_ids, 0)
    id_recv[hist, pl.ds(me, 1), :] = id_send[pl.ds(me, 1), :]

    def exchange(send, recv, sem, t):
        def step(i, carry):
            peer = lax.rem(me + i, ENT)
            remote(send.at[t, peer], recv.at[t, me], sem.at[0, t], sem.at[1, t], {"ent": peer})
            return carry

        lax.fori_loop(1, ENT, step, 0)
        recv[t, me] = send[t, me]

    others = pl.ds(0, ENT - 1)

    for i in range(6, len(fetched)):
        fetched[i].wait()
    rel_block[NREL // 16 * 16 :, :] = jnp.zeros((REL_PAD - NREL // 16 * 16, HALF), bf16)
    rel_block[:NREL, :] = relation[:, pl.ds(pl.multiple_of(block * HALF, HALF), HALF)]

    q_parts = split3(query_grad[...])
    hot_query = hot(iota((ROWS, 128), 0) == query_ent[...])
    cot[...] = nn(hot_query, q_parts[0]) + (nn(hot_query, q_parts[1]) + nn(hot_query, q_parts[2]))
    hot_query = hot(iota((REL_PAD, 128), 0) == query_rel[...])
    by_query = nn(hot_query, q_parts[0]) + (nn(hot_query, q_parts[1]) + nn(hot_query, q_parts[2]))
    for g in range(ENT):
        c, xx, zz = g // GROUP, g // ZS % XS, g % ZS
        at = c * GROUP + zz * XS + xx
        grads1[at, R_QUERY : R_QUERY + 8, :] = by_query[g * 8 : (g + 1) * 8, :]
    grads2[GROUP:, R_NEIGH : R_NEIGH + 8, :] = jnp.zeros((GROUP, 8, QUART), f32)

    def forward_messages(t):
        @pl.when(hist != t)
        def _():
            wait_bytes(ids.at[t], ids_sem.at[1, t])
            wait_bytes(states.at[t, block], st_sem.at[1 + block, t])

        if t == top:
            for later in range(t - 1, -1, -1):
                share_states(later)
        hot_src_t[t] = hot(iota((ROWS, SLOTS), 0) == ids[t, 0:1, :])
        hot_rel_t[t] = hot(iota((REL_PAD, SLOTS), 0) == ids[t, 1:2, :])
        inputs[t] = (
            tn(hot_src_t[t], states[t, block]) + tn(hot_rel_t[t], rel_block[...])
        ).astype(bf16)
        f_send[t] = pack(nn(inputs[t], w_cols[...]))
        exchange(f_send, f_recv, f_sem, t)

    def forward_rest(t):
        @pl.when(hist != t)
        def _():
            wait_bytes(states.at[t, 1 - block], st_sem.at[2 - block, t])

        logit = nn(states[t, 0], w_gate[:HALF, :]) + nn(states[t, 1], w_gate[HALF:, :])
        dense = nn(states[t, 0], w_self[:HALF, :]) + nn(states[t, 1], w_self[HALF:, :])
        opened = jax.nn.sigmoid(logit + b_gate[...])
        shut = 1.0 - opened

        @pl.when(hist != t)
        def _():
            wait_bytes(id_recv.at[t], fwd_id_sem.at[1, t])

        to_slot = hot((iota((SLOTS, ENT), 0) >> 3) == iota((SLOTS, ENT), 1))
        arrived = nn(to_slot, id_recv[t].astype(bf16))
        arrived = jnp.where(
            iota((SLOTS, 128), 1) == (iota((SLOTS, 128), 0) & 7), arrived, 0.0
        ).astype(bf16)
        ones = jnp.ones((ROWS, 128), bf16)
        hot_dst[t] = hot(nt(arrived, ones) == iota((SLOTS, ROWS), 1).astype(f32))
        hot_dst_t = hot(nt(ones, arrived) == iota((ROWS, SLOTS), 0).astype(f32))
        degree = nn(hot_dst_t, jnp.ones((SLOTS, QUART), bf16))
        scale = 1.0 / jnp.maximum(degree, 1.0)
        scaling[t] = scale
        wait_bytes(f_recv.at[t, others], f_sem.at[1, t])
        pre_act = nn(hot_dst_t, unpack(f_recv[t])) * scale + dense
        sig = jax.nn.sigmoid(pre_act)
        keep[t] = shut
        own = states[t, block, :, near].astype(f32)
        coef_gate[t] = (pre_act * sig - own) * opened * shut
        coef_pre[t] = opened * (sig * (1.0 + pre_act * (1.0 - sig)))

    forward_messages(top)
    wait_bytes(id_recv.at[hist, others], id_sem.at[1])
    for i in range(1, HIST):
        remote(
            id_recv.at[hist],
            id_recv.at[hist],
            fwd_id_sem.at[0, hist],
            fwd_id_sem.at[1, hist],
            {"hist": lax.rem(hist + i, HIST)},
        )
    forward_rest(top)

    def add_grads(ref, at, value, t, owners=ENT):
        if t == top:
            ref[:owners, at : at + 8, :] = by_shard(value)
        else:
            ref[:owners, at : at + 8, :] += by_shard(value)

    def returned_grads(t):
        back = unpack(b_recv[t])
        add_grads(grads2, R_NEIGH, tn(inputs[t], back), t, GROUP)
        add_grads(grads2, R_REL, nn(hot_rel_t[t], back), t)

    partner = me + 1 - 2 * core
    mine = pl.multiple_of(core * GROUP, GROUP)
    half = pl.ds(mine, GROUP)
    other_half = pl.ds(pl.multiple_of((1 - core) * GROUP, GROUP), GROUP)

    def along_x(src, dst, sem):
        copies = []
        for i in range(1, XS):
            there = lax.rem(x + i, XS)
            where = {"ent": me + (there - x) * (CORES * ZS)}
            copies.append(remote(src(there), dst, sem.at[0, i], sem.at[1, i], where))
        return copies

    def along_z(src, dst, sem):
        copies = []
        for i in range(1, ZS):
            there = lax.rem(z + i, ZS)
            where = {"ent": me + (there - z) * CORES}
            copies.append(remote(src(there), dst, sem.at[0, i], sem.at[1, i], where))
        return copies

    def along_hist(src, dst, sem):
        copies = []
        for i in range(1, HIST):
            where = {"hist": lax.rem(hist + i, HIST)}
            copies.append(remote(src, dst, sem.at[0, i], sem.at[1, i], where))
        return copies

    def to_core(src, dst, sem, i):
        return remote(src, dst, sem.at[0, i], sem.at[1, i], {"ent": partner})

    def finish(copies):
        for copy in copies:
            copy.wait()

    for t in range(top, -1, -1):
        c = cot[...]
        pre_term = c * coef_pre[t]
        b_send[t] = pack(nn(hot_dst[t], (pre_term * scaling[t]).astype(bf16)))
        exchange(b_send, b_recv, b_sem, t)
        gate_term = c * coef_gate[t]
        gate_low = gate_term.astype(bf16)
        pre_low = pre_term.astype(bf16)
        for j in range(4):
            rows = slice(j * QUART, (j + 1) * QUART)
            piece = nt(gate_low, w_gate[rows, :]) + nt(pre_low, w_self[rows, :])
            part[j] = piece
            part_send[t, j] = piece.astype(bf16)
        for i in range(1, HIST):
            there = lax.rem(hist + i, HIST)
            remote(
                part_send.at[t, there],
                part_recv.at[t, hist],
                part_sem.at[0, t],
                part_sem.at[1, t],
                {"hist": there},
            )
        if t == top:
            forward_messages(t - 1)
        if t > 1:
            forward_messages(t - 2)
        down = jnp.sum(gate_term, axis=0, keepdims=True)
        bias[...] = down if t == top else bias[...] + down
        lows = jnp.concatenate([gate_low, pre_low], axis=1)
        total = jnp.concatenate([tn(states[t, 0], lows), tn(states[t, 1], lows)], axis=0)
        add_grads(grads1, R_GATE, total[:, :QUART], t)
        add_grads(grads1, R_SELF, total[:, QUART:], t)
        if t == 0:
            row = R_QUERY + BIAS_ROW % 8
            grads1[BIAS_ROW // 8, row : row + 1, :] = bias[...]
            core1 = to_core(grads1.at[other_half], core_recv1, core_sem, 0)
        if t < top:
            returned_grads(t + 1)
        if t == 0:
            core1.wait()
            both = (grads1[half] + core_recv1[...]).reshape(ZS, XS, ROWS1, QUART)
            sum1[...] = both
            for xx in range(XS):
                x_send1[xx] = both[:, xx].astype(bf16)
            x1 = along_x(lambda there: x_send1.at[there], x_recv1.at[x], x1_sem)

        if 0 < t < top:
            forward_rest(t - 1)
        wait_bytes(b_recv.at[t, others], b_sem.at[1, t])
        high, low = split(nn(hot_src_t[t], unpack(b_recv[t])))
        sum_send[t] = high
        remote(
            sum_send.at[t], sum_recv.at[t], sum_sem.at[0, t], sum_sem.at[1, t], {"hist": mate}
        )
        near_part = nt(high, w_own[...]) + nt(low, w_own[...]) + c * keep[t] + part[hist]
        if t == top:
            forward_rest(t - 1)
        if t == 0:
            returned_grads(0)
            core2 = to_core(grads2.at[other_half], core_recv2, core_sem, 1)
            finish(x1)
            total = sum1[:, x]
            for i in range(1, XS):
                total = total + x_recv1[lax.rem(x + i, XS)].astype(f32)
            z_send1[...] = total
            z1 = along_z(lambda there: z_send1.at[there], z_recv1.at[z], z1_sem)
        wait_bytes(part_recv.at[t, pl.ds(0, HIST - 1)], part_sem.at[1, t])
        for i in range(1, HIST):
            near_part = near_part + part_recv[t, lax.rem(hist + i, HIST)].astype(f32)
        wait_bytes(sum_recv.at[t], sum_sem.at[1, t])
        c = near_part + nt(sum_recv[t], w_other[...])
        cot[...] = c
        res_send[t] = c.astype(bf16)

        @pl.when(hist == t)
        def _():
            result[t] = res_send[t]

        @pl.when(hist != t)
        def _():
            remote(
                res_send.at[t],
                result.at[hist],
                res_sem.at[0],
                res_sem.at[1],
                {"hist": t},
            )

    core2.wait()
    both = (grads2[half] + core_recv2[...]).reshape(XS, ZS, ROWS2, QUART)
    sum2[...] = both
    x_send2[...] = both.astype(bf16)
    x2 = along_x(lambda there: x_send2.at[there], x_recv2.at[x], x2_sem)

    finish(z1)
    shard1 = z_send1[z]
    for i in range(1, ZS):
        shard1 = shard1 + z_recv1[lax.rem(z + i, ZS)]
    place1 = mine + z * XS + x
    gathered1[hist, place1] = shard1[:KEPT, :].astype(bf16)
    own1 = gathered1.at[hist, place1]
    gx1 = along_x(lambda there: own1, own1, gx1_sem)
    place2 = mine + x * ZS + z
    gathered4[place2, hist] = shard1[R_SELF : R_SELF + 8, :].astype(bf16)
    own4 = gathered4.at[place2, hist]
    gy4 = along_hist(own4, own4, gy4_sem)

    finish(x2)
    total = sum2[x]
    for i in range(1, XS):
        total = total + x_recv2[lax.rem(x + i, XS)].astype(f32)
    z_send2[...] = total
    z2 = along_z(lambda there: z_send2.at[there], z_recv2.at[z], z2_sem)

    finish(gx1)
    line1 = gathered1.at[hist, pl.ds(mine + z * XS, XS)]
    gz1 = along_z(lambda there: line1, line1, gz1_sem)
    finish(gy4)
    all4 = gathered4.at[place2]
    gz4 = along_z(lambda there: all4, all4, gz4_sem)

    finish(z2)
    shard2 = z_send2[z]
    for i in range(1, ZS):
        shard2 = shard2 + z_recv2[lax.rem(z + i, ZS)]
    y_recv2[hist] = jnp.concatenate([shard2[R_REL:, :], shard1[R_QUERY:, :]], axis=0)
    y2 = along_hist(y_recv2.at[hist], y_recv2.at[hist], y2_sem)
    gathered3[hist, place1] = shard2[:R_REL, :].astype(bf16)
    own3 = gathered3.at[hist, place1]
    gx3 = along_x(lambda there: own3, own3, gx3_sem)

    finish(gz1)
    plane1 = gathered1.at[hist, half]
    last = [to_core(plane1, plane1, gc1_sem, 0)]
    gy1 = along_hist(plane1, plane1, gy1_sem)
    finish(gz4)
    line4 = gathered4.at[pl.ds(mine + x * ZS, ZS)]
    gx4 = along_x(lambda there: line4, line4, gx4_sem)
    last.append(to_core(line4, line4, gc4_sem, 0))

    finish(y2)
    for b in range(2):
        wide = jnp.concatenate([y_recv2[2 * b, :8, :], y_recv2[2 * b + 1, :8, :]], axis=1)
        high = wide.astype(bf16).astype(f32)
        twice = nt(jnp.concatenate([high, wide - high], axis=0).astype(bf16), w_neigh[b])
        by_rel = twice[:8, :] + twice[8:, :]
        for j in range(2):
            h = 2 * b + j
            rel_rows = by_rel[:, j * QUART : (j + 1) * QUART] + y_recv2[h, 8:, :]
            gathered2[place2, h] = rel_rows.astype(bf16)
    own2 = gathered2.at[place2]
    gz2 = along_z(lambda there: own2, own2, gz2_sem)
    finish(gx3)
    line3 = gathered3.at[hist, pl.ds(mine + z * XS, XS)]
    gz3 = along_z(lambda there: line3, line3, gz3_sem)
    finish(gz2)
    line2 = gathered2.at[pl.ds(mine + x * ZS, ZS)]
    gx2 = along_x(lambda there: line2, line2, gx2_sem)
    last.append(to_core(line2, line2, gc2_sem, 0))
    finish(gz3)
    plane3 = gathered3.at[hist, half]
    gy3 = along_hist(plane3, plane3, gy3_sem)
    last.append(to_core(plane3, plane3, gc3_sem, 0))
    for i in range(1, HIST):
        gy1[i - 1].wait()
        came = gathered1.at[lax.rem(hist + HIST - i, HIST), half]
        last.append(to_core(came, came, gc1_sem, i))
    for i in range(1, XS):
        gx4[i - 1].wait()
        came = gathered4.at[pl.ds(mine + lax.rem(x + XS - i, XS) * ZS, ZS)]
        last.append(to_core(came, came, gc4_sem, i))
    for i in range(1, XS):
        gx2[i - 1].wait()
        came = gathered2.at[pl.ds(mine + lax.rem(x + XS - i, XS) * ZS, ZS)]
        last.append(to_core(came, came, gc2_sem, i))
    for i in range(1, HIST):
        gy3[i - 1].wait()
        came = gathered3.at[lax.rem(hist + HIST - i, HIST), half]
        last.append(to_core(came, came, gc3_sem, i))
    finish(last)

    three = pl.ds(0, HIST - 1)
    wait_bytes(result.at[three], res_sem.at[1])
    wait_bytes(res_send.at[three], res_sem.at[0])
    wait_bytes(id_send.at[others], id_sem.at[0])
    wait_bytes(id_recv.at[three], fwd_id_sem.at[0, hist])
    wait_bytes(ids.at[three], ids_sem.at[0, hist])
    wait_bytes(states.at[three], st_sem.at[0, hist])
    for t in range(HIST):
        wait_bytes(f_send.at[t, others], f_sem.at[0, t])
        wait_bytes(b_send.at[t, others], b_sem.at[0, t])
        wait_bytes(part_send.at[t, three], part_sem.at[0, t])
        wait_bytes(sum_send.at[t], sum_sem.at[0, t])


def unfold(
    factor,
    gathered1_in,
    gathered2_in,
    gathered3_in,
    gathered4_in,
    result_in,
    out_states,
    out_neigh,
    out_self,
    out_gate,
    out_bias,
    out_rel,
    gathered1,
    gathered2,
    gathered3,
    gathered4,
    result,
    new_states,
    new_neigh,
    new_self,
    new_gate,
    new_bias,
    new_rel,
    in_sem,
    out_sem,
):
    fetched = []
    for src, dst in (
        (gathered1_in, gathered1),
        (result_in, result),
        (gathered2_in, gathered2),
        (gathered3_in, gathered3),
        (gathered4_in, gathered4),
    ):
        fetched.append(pltpu.make_async_copy(src, dst, in_sem.at[len(fetched)]))
        fetched[-1].start()
    stored = []

    def store(src, dst):
        stored.append(pltpu.make_async_copy(src, dst, out_sem.at[len(stored)]))
        stored[-1].start()

    fetched[0].wait()
    for h in range(HIST):
        rows = gathered1[h].astype(f32) * factor
        new_gate[:, h * QUART : (h + 1) * QUART] = rows.reshape(D, QUART)
    store(new_gate, out_gate)
    fetched[1].wait()
    for h in range(HIST):
        new_states[0, :, h * QUART : (h + 1) * QUART] = result[h].astype(f32)
    store(new_states, out_states)
    fetched[2].wait()
    for h in range(HIST):
        lanes = slice(h * QUART, (h + 1) * QUART)
        by_rel = (gathered2[:, h].astype(f32) * factor).reshape(REL_PAD, QUART)
        new_rel[:, lanes] = by_rel[:NREL, :]
        new_bias[:, lanes] = by_rel[BIAS_ROW : BIAS_ROW + 1, :]
    store(new_rel, out_rel)
    fetched[3].wait()
    for h in range(HIST):
        lanes = slice((h % 2) * QUART, (h % 2 + 1) * QUART)
        rows = gathered3[h, :GROUP].astype(f32) * factor
        for g in range(GROUP):
            at = g % ZS * XS + g // ZS
            new_neigh[h // 2, g * 8 : (g + 1) * 8, lanes] = rows[at]
    store(new_neigh, out_neigh)
    fetched[4].wait()
    for h in range(HIST):
        rows = gathered4[:, h].astype(f32) * factor
        for g in range(ENT):
            at = g // GROUP * GROUP + g % XS * ZS + g % GROUP // XS
            new_self[g * 8 : (g + 1) * 8, h * QUART : (h + 1) * QUART] = rows[at]
    store(new_self, out_self)
    store(new_bias, out_bias)
    for copy in stored:
        copy.wait()


def on_device(
    states,
    w_neigh,
    w_self,
    w_gate,
    b_gate,
    relation,
    edge_src,
    edge_rel,
    edge_dst,
    send_counts,
    query_ent,
    query_rel,
    query_grad,
):
    factor = 1.0 / math.sqrt(HIST * ENT * ROWS)
    vmem = pl.BlockSpec(memory_space=pltpu.VMEM)
    anywhere = pl.BlockSpec(memory_space=pl.ANY)
    dma = pltpu.SemaphoreType.DMA
    shape = jax.ShapeDtypeStruct
    v = pltpu.VMEM
    i32 = jnp.int32
    gathered1, gathered2, gathered3, gathered4, result = pl.pallas_call(
        kernel,
        out_shape=(
            shape((HIST, ENT, KEPT, QUART), bf16),
            shape((ENT, HIST, 8, QUART), bf16),
            shape((HIST, ENT, 8, QUART), bf16),
            shape((ENT, HIST, 8, QUART), bf16),
            shape((HIST, ROWS, QUART), bf16),
        ),
        in_specs=[anywhere] * 13,
        out_specs=(vmem,) * 5,
        scratch_shapes=[
            v((HIST, 2, ROWS, HALF), bf16),
            v((HALF, QUART), bf16),
            v((QUART, QUART), bf16),
            v((QUART, QUART), bf16),
            v((D, QUART), bf16),
            v((D, QUART), bf16),
            v((1, QUART), f32),
            v((NREL, D), bf16),
            v((HIST, 8, SLOTS), i32),
            v((1, SLOTS), i32),
            v((1, ENT), i32),
            v((1, 128), i32),
            v((1, 128), i32),
            v((128, QUART), f32),
            v((ENT, 128), f32),
            v((HIST, ENT, 128), f32),
            v((REL_PAD, HALF), bf16),
            v((HIST, SLOTS, HALF), bf16),
            v((HIST, ROWS, SLOTS), bf16),
            v((HIST, REL_PAD, SLOTS), bf16),
            v((HIST, SLOTS, ROWS), bf16),
            v((HIST, ENT, 8, QUART), bf16),
            v((HIST, ENT, 8, QUART), bf16),
            v((HIST, ENT, 8, QUART), bf16),
            v((HIST, ENT, 8, QUART), bf16),
            v((ROWS, QUART), f32),
            v((HIST, ROWS, QUART), f32),
            v((HIST, ROWS, QUART), f32),
            v((HIST, ROWS, QUART), f32),
            v((HIST, ROWS, QUART), f32),
            v((1, QUART), f32),
            v((HIST, ROWS, QUART), f32),
            v((HIST, HIST, ROWS, QUART), bf16),
            v((HIST, HIST, ROWS, QUART), bf16),
            v((HIST, ROWS, QUART), bf16),
            v((HIST, ROWS, QUART), bf16),
            v((HIST, ROWS, QUART), bf16),
            v((2, HALF, HALF), bf16),
            v((ENT, ROWS1, QUART), f32),
            v((GROUP, ROWS1, QUART), f32),
            v((ZS, XS, ROWS1, QUART), f32),
            v((XS, ZS, ROWS1, QUART), bf16),
            v((XS, ZS, ROWS1, QUART), bf16),
            v((ZS, ROWS1, QUART), f32),
            v((ZS, ROWS1, QUART), f32),
            v((ENT, ROWS2, QUART), f32),
            v((GROUP, ROWS2, QUART), f32),
            v((XS, ZS, ROWS2, QUART), f32),
            v((XS, ZS, ROWS2, QUART), bf16),
            v((XS, ZS, ROWS2, QUART), bf16),
            v((ZS, ROWS2, QUART), f32),
            v((ZS, ROWS2, QUART), f32),
            v((HIST, 16, QUART), f32),
            dma((17,)),
            dma((2,)),
            dma((2, HIST)),
            dma((3, HIST)),
            dma((2, HIST)),
            dma((2, HIST)),
            dma((2, HIST)),
            dma((2, HIST)),
            dma((2, HIST)),
            dma((2,)),
            dma((2, 2)),
            dma((2, XS)),
            dma((2, ZS)),
            dma((2, XS)),
            dma((2, ZS)),
            dma((2, HIST)),
            dma((2, XS)),
            dma((2, ZS)),
            dma((2, HIST)),
            dma((2, HIST)),
            dma((2, ZS)),
            dma((2, XS)),
            dma((2, XS)),
            dma((2, XS)),
            dma((2, ZS)),
            dma((2, HIST)),
            dma((2, HIST)),
            dma((2, HIST)),
            dma((2, ZS)),
            dma((2, XS)),
            dma((2, XS)),
        ],
        compiler_params=pltpu.CompilerParams(
            collective_id=0, has_side_effects=True, vmem_limit_bytes=54 << 20
        ),
        name="encoder_backward",
    )(
        states,
        w_neigh,
        w_self,
        w_gate,
        b_gate.reshape(1, D),
        relation,
        edge_src,
        edge_rel,
        edge_dst,
        send_counts,
        query_ent.reshape(1, 128),
        query_rel.reshape(1, 128),
        query_grad,
    )
    result, grad_neigh, grad_self, grad_gate, grad_bias, grad_rel = pl.pallas_call(
        functools.partial(unfold, factor),
        out_shape=(
            shape((1, ROWS, D), f32),
            shape((2, HALF, HALF), f32),
            shape((D, D), f32),
            shape((D, D), f32),
            shape((1, D), f32),
            shape((NREL, D), f32),
        ),
        in_specs=[anywhere] * 5,
        out_specs=(anywhere,) * 6,
        scratch_shapes=[
            v((HIST, ENT, KEPT, QUART), bf16),
            v((ENT, HIST, 8, QUART), bf16),
            v((HIST, ENT, 8, QUART), bf16),
            v((ENT, HIST, 8, QUART), bf16),
            v((HIST, ROWS, QUART), bf16),
            v((1, ROWS, D), f32),
            v((2, HALF, HALF), f32),
            v((D, D), f32),
            v((D, D), f32),
            v((1, D), f32),
            v((NREL, D), f32),
            dma((5,)),
            dma((6,)),
        ],
        compiler_params=pltpu.CompilerParams(vmem_limit_bytes=54 << 20),
        name="unfold",
    )(gathered1, gathered2, gathered3, gathered4, result)
    return result, grad_neigh, grad_self, grad_gate, grad_bias.reshape(D), grad_rel


def solution(mesh):
    return jax.shard_map(
        on_device,
        mesh=mesh,
        in_specs=(
            P("hist", "ent", None),
            P(),
            P(),
            P(),
            P(),
            P(),
            P("hist", "ent"),
            P("hist", "ent"),
            P("hist", "ent"),
            P("hist", "ent"),
            P("ent"),
            P("ent"),
            P("ent", None),
        ),
        out_specs=(P("hist", "ent", None), P(), P(), P(), P(), P()),
        check_vma=False,
    )
```
